32 devices in a mesh: table: 8 (over z, core), seq: 4 (over y, x).
Axes of the slice: x: 2, y: 2, z: 4, core: 2. Of those that a mesh axis runs over, the one named last changes fastest.
Arguments:
- item_ids: int32 [32768], P('seq'), may hold values from 0 to 131071, as said below
- item_table: bfloat16 [131072, 512], P('seq', 'table'), may hold values from -6 to 6
- group_counts: int32 [8, 4, 8], replicated, may hold values from 0 to 192, as said below
- lengths: int32 [8], replicated, may hold values from 128 to 512
- history: bfloat16 [8, 2, 2, 512, 512], P('table', None, None, 'seq'), may hold values from -6 to 6
- w_in: bfloat16 [512, 2048], replicated, may hold values from -0.25 to 0.25
- w_out: bfloat16 [2048, 512], replicated, may hold values from -0.125 to 0.125
- w_proj: bfloat16 [2, 512, 1024], replicated, may hold values from -0.25 to 0.25
- w_back: bfloat16 [2, 512, 512], replicated, may hold values from -0.25 to 0.25
Outputs:
- ranked_states: bfloat16 [49152, 512], P(('table', 'seq'))
The draws below stay inside these ranges and needn't reach their ends.
Inputs may be any that keep to these rules, and one draw needn't show every extreme that they name: `item_ids`: the ids of the 8192 candidates of index s of seq lie in s * 32768 to (s + 1) * 32768 - 1. Each group_counts[t, s, :] sums to 1024; every sender has some entry equal to 192; on some index s every t sends 192 to one group.
All inputs are finite; a program needn't handle non-finite values.
Results may differ from the reference program's by a relative error of at most 0.013.
Values may be sent and summed in bfloat16 or wider, within the bound.
No kernel may reach another device: no remote copies, remote signals or barrier semaphores. Data moves between devices by JAX's collectives and lax.ppermute only.
A program may use at most 128 MiB of HBM per device.

```python
import jax
import jax.numpy as jnp
from jax import lax

D = 512
FF = 2048
HEADS = 8
HEAD_DIM = 64
LAYERS = 2
HIST = 512
VOCAB_DEV = 32768
ROWS = 1024
GROUPS = 8
SHARDS = 4
CAP = 192
VOCAB = 131072
ROWS_SEQ = 8192
ROWS_ALL = 32768
SLOTS_ALL = 49152


def draw_item_ids(key, part):
    owner = jnp.arange(ROWS_ALL, dtype=jnp.int32) // ROWS_SEQ
    local_ids = jax.random.randint(key, (ROWS_ALL,), 0, VOCAB_DEV, dtype=jnp.int32)
    drawn = owner * VOCAB_DEV + local_ids
    return drawn.at[0].set(0).at[ROWS_ALL - 1].set(VOCAB - 1)


def draw_group_counts(key, part):
    pick_key, spot_key, walk_key = jax.random.split(jax.random.fold_in(key, 11), 3)
    senders = GROUPS * SHARDS
    full_at = jax.random.randint(pick_key, (GROUPS, SHARDS), 0, GROUPS, dtype=jnp.int32)
    spot_pair = jax.random.randint(spot_key, (2,), 0, GROUPS * SHARDS, dtype=jnp.int32)
    spot_group = spot_pair[0] % GROUPS
    spot_shard = spot_pair[1] % SHARDS
    full_at = jnp.where(jnp.arange(SHARDS, dtype=jnp.int32)[None, :] == spot_shard, spot_group, full_at).reshape(senders)
    columns = jnp.arange(GROUPS, dtype=jnp.int32)[None, :]
    position = jnp.where(columns < full_at[:, None], columns, columns - 1)
    remain = ROWS - CAP
    even_share = remain // (GROUPS - 1)
    leftover = remain - even_share * (GROUPS - 1)
    initial = jnp.where(columns == full_at[:, None], CAP, even_share + (position < leftover).astype(jnp.int32))
    steps_total = 4 * ROWS
    walk_pairs = jax.random.randint(walk_key, (steps_total, 2, senders), 0, GROUPS, dtype=jnp.int32)

    def walk_step(step_num, current):
        giver_col = walk_pairs[step_num, 0]
        taker_col = walk_pairs[step_num, 1]
        give_hot = (columns == giver_col[:, None]).astype(jnp.int32)
        take_hot = (columns == taker_col[:, None]).astype(jnp.int32)
        give_have = jnp.sum(current * give_hot, axis=1)
        take_have = jnp.sum(current * take_hot, axis=1)
        allowed = (giver_col != full_at) & (taker_col != full_at) & (giver_col != taker_col) & (give_have > 0) & (take_have < CAP)
        move_mask = allowed.astype(jnp.int32)[:, None]
        return current - move_mask * give_hot + move_mask * take_hot
    walked = lax.fori_loop(0, steps_total, walk_step, initial)
    return walked.reshape(GROUPS, SHARDS, GROUPS)


def draw_lengths(key, part):
    draw_key, pick_key = jax.random.split(jax.random.fold_in(key, 23), 2)
    drawn = jax.random.randint(draw_key, (GROUPS,), HIST // 4, HIST + 1, dtype=jnp.int32)
    picks = jax.random.randint(pick_key, (2,), 0, GROUPS, dtype=jnp.int32)
    longest = picks[0]
    shortest = (picks[0] + 1 + picks[1] % (GROUPS - 1)) % GROUPS
    return drawn.at[longest].set(HIST).at[shortest].set(HIST // 4)


def steps_of(stream_key, dims, cuts, least, top_value):
    gain = 1.0
    for axis_at, parts in cuts:
        heights = jax.random.uniform(jax.random.fold_in(jax.random.fold_in(stream_key, 6), axis_at), (parts,), jnp.float32, least / len(cuts), top_value / len(cuts))
        gain = gain * jnp.repeat(jnp.exp(heights), dims[axis_at] // parts).reshape((-1,) + (1,) * (len(dims) - 1 - axis_at))
    return gain


def bell_draw(stream_key, extent, deviation, bound, pieces=(), held_as=jnp.bfloat16):
    loudness = steps_of(stream_key, extent, pieces, -0.22, 0.18) if pieces else 1.0
    values = jax.random.normal(stream_key, extent, jnp.float32) * deviation * loudness
    return jnp.minimum(jnp.maximum(values, -bound), bound).astype(held_as)


def setup_inputs(seed: int = 0) -> dict:
    key_list = jax.random.split(jax.random.key(seed), 10)
    item_ids = draw_item_ids(jax.random.fold_in(key_list[9], 71), 0)
    item_table = bell_draw(key_list[1], (VOCAB, D), 1.0, 6.0, ((0, 4), (1, 8)))
    group_counts = draw_group_counts(jax.random.fold_in(key_list[9], 71), 0)
    lengths = draw_lengths(jax.random.fold_in(key_list[9], 71), 0)
    history = bell_draw(key_list[4], (GROUPS, LAYERS, 2, HIST, D), 1.0, 6.0, ((0, 8), (3, 4)))
    w_in = bell_draw(key_list[5], (D, FF), D ** -0.5, 0.25)
    w_out = bell_draw(key_list[6], (FF, D), FF ** -0.5, 0.125)
    w_proj = bell_draw(key_list[7], (LAYERS, D, 2 * D), D ** -0.5, 0.25)
    w_back = bell_draw(key_list[8], (LAYERS, D, D), D ** -0.5, 0.25)
    return dict(item_ids=item_ids, item_table=item_table, group_counts=group_counts, lengths=lengths, history=history, w_in=w_in, w_out=w_out, w_proj=w_proj, w_back=w_back)


def layer_norm(values):
    row_mean = lax.optimization_barrier(jnp.mean(values, axis=-1, keepdims=True))
    centred = values - row_mean
    variance = lax.optimization_barrier(jnp.mean(centred * centred, axis=-1, keepdims=True))
    return centred * lax.rsqrt(variance + 1e-06)

def stored(values):
    return lax.optimization_barrier(values.astype(jnp.bfloat16)).astype(jnp.float32)

def attend_layer(states, layer_cache, key_mask, w_proj, w_back):
    row_count = states.shape[0]
    normed = layer_norm(states.astype(jnp.float32)).astype(jnp.bfloat16)
    projected = jax.nn.silu(jnp.dot(normed, w_proj, preferred_element_type=jnp.float32))
    gate = projected[:, :D]
    queries = stored(projected[:, D:]).reshape(row_count, HEADS, HEAD_DIM)
    key_heads = layer_cache[0].astype(jnp.float32).reshape(HIST, HEADS, HEAD_DIM)
    value_heads = layer_cache[1].astype(jnp.float32).reshape(HIST, HEADS, HEAD_DIM)
    scores = jnp.einsum('qhd,khd->hqk', queries, key_heads) * HEAD_DIM ** (-0.5)
    weights = stored(jnp.where(key_mask[None, None, :], jax.nn.silu(scores), 0.0))
    attended = jnp.einsum('hqk,khd->qhd', weights, value_heads).reshape(row_count, D)
    mixed_rows = (layer_norm(attended) * gate).astype(jnp.bfloat16)
    return (states.astype(jnp.float32) + jnp.dot(mixed_rows, w_back, preferred_element_type=jnp.float32)).astype(jnp.bfloat16)

def reference(item_ids, item_table, group_counts, lengths, history, w_in, w_out, w_proj, w_back):
    embedded = jnp.take(item_table, item_ids, axis=0)
    hidden = jax.nn.silu(jnp.dot(embedded, w_in, preferred_element_type=jnp.float32)).astype(jnp.bfloat16)
    content = (embedded.astype(jnp.float32) + jnp.dot(hidden, w_out, preferred_element_type=jnp.float32)).astype(jnp.bfloat16)
    offsets = jnp.cumsum(group_counts, axis=2) - group_counts
    slot_ids = jnp.arange(CAP, dtype=jnp.int32)
    shard_ids = jnp.arange(SHARDS, dtype=jnp.int32)[:, None, None]
    table_ids = jnp.arange(GROUPS, dtype=jnp.int32)[None, :, None]

    def one_group(group_id):
        counts_here = group_counts[:, :, group_id].T
        offsets_here = offsets[:, :, group_id].T
        source = shard_ids * ROWS_SEQ + table_ids * ROWS + offsets_here[:, :, None] + slot_ids[None, None, :]
        source = jnp.minimum(source, ROWS_ALL - 1).astype(jnp.int32)
        filled = slot_ids[None, None, :] < counts_here[:, :, None]
        picked = jnp.take(content, source.reshape(-1), axis=0)
        states = jnp.where(filled.reshape(-1, 1), picked, jnp.zeros((), jnp.bfloat16))
        group_cache = history[group_id]
        key_mask = jnp.arange(HIST, dtype=jnp.int32) < lengths[group_id]

        def run_block(block_states):
            for layer_num in range(LAYERS):
                block_states = attend_layer(block_states, group_cache[layer_num], key_mask, w_proj[layer_num], w_back[layer_num])
            return block_states
        return lax.map(run_block, states.reshape(SHARDS, GROUPS * CAP, D))
    result = lax.map(one_group, jnp.arange(GROUPS, dtype=jnp.int32))
    return result.reshape(SLOTS_ALL, D)
```

```python
import functools

import jax
import jax.numpy as jnp
from jax import lax
from jax.experimental import pallas as pl
from jax.experimental.pallas import tpu as pltpu
from jax.sharding import PartitionSpec as P

HEADS = 8
LANES = 128
MIB = 1 << 20
ANY = pl.BlockSpec(memory_space=pl.ANY)
SMEM = pl.BlockSpec(memory_space=pltpu.SMEM)
VMEM = pl.BlockSpec(memory_space=pltpu.VMEM)


def lookup_kernel(geometry, ids, counts, table_t, out, rows_major, picked):
    groups, row_count, total, packing, tile = geometry
    columns, vocab = table_t.shape
    shard = lax.axis_index("seq")
    first_id = shard * vocab
    eye = (
        lax.broadcasted_iota(jnp.int32, (columns, LANES), 0)
        == lax.broadcasted_iota(jnp.int32, (columns, LANES), 1) % columns
    ).astype(jnp.bfloat16)
    block = min(vocab, 2048)

    def turn(step, carry):
        at = pl.multiple_of(step * block, block)
        rows_major[pl.ds(at, block), :] = lax.dot_general(
            table_t[:, pl.ds(at, block)],
            eye,
            (((0,), (0,)), ((), ())),
            preferred_element_type=jnp.float32,
        )
        return carry

    lax.fori_loop(0, vocab // block, turn, 0)

    def gather_rows(group, source, target, amount):
        def row(offset):
            picked[group, pl.ds(target + offset, 1), :] = rows_major[
                pl.ds(ids[source + offset] - first_id, 1), :
            ]

        return row

    def sender(sender_id, starts):
        source = sender_id * row_count
        new_starts = []
        for group in range(groups):
            amount = counts[sender_id, shard, group]
            target = starts[group]

            def eight(step, carry, group=group, source=source, target=target):
                for k in range(8):
                    picked[group, pl.ds(target + step * 8 + k, 1), :] = rows_major[
                        pl.ds(ids[source + step * 8 + k] - first_id, 1), :
                    ]
                return carry

            def one(step, carry, group=group, source=source, target=target):
                picked[group, pl.ds(target + step, 1), :] = rows_major[
                    pl.ds(ids[source + step] - first_id, 1), :
                ]
                return carry

            last = (sender_id == groups - 1) & (group == groups - 1)
            rounds = jnp.where(last, amount // 8, (amount + 7) // 8)
            lax.fori_loop(0, rounds, eight, 0)
            lax.fori_loop(rounds * 8, jnp.where(last, amount, 0), one, 0)
            source = source + amount
            new_starts.append(target + amount)
        return tuple(new_starts)

    lax.fori_loop(0, groups, sender, (jnp.int32(0),) * groups)

    part = tile // packing
    lane = lax.broadcasted_iota(jnp.int32, (part, LANES), 1) // columns

    def pack(group, carry):
        for step in range(total // tile):
            value = picked[group, pl.ds(step * tile, part), :]
            for piece in range(1, packing):
                value = jnp.where(
                    lane == piece,
                    picked[group, pl.ds(step * tile + piece * part, part), :],
                    value,
                )
            out[group, pl.ds(step * part, part), :] = value.astype(jnp.bfloat16)
        return carry

    lax.fori_loop(0, groups, pack, 0)


def lookup(ids, counts, table_t, groups, total, packing, tile):
    columns, vocab = table_t.shape
    geometry = (groups, ids.shape[0] // groups, total, packing, tile)
    return pl.pallas_call(
        functools.partial(lookup_kernel, geometry),
        out_shape=jax.ShapeDtypeStruct((groups, total // packing, LANES), jnp.bfloat16),
        in_specs=[SMEM, SMEM, VMEM],
        out_specs=VMEM,
        scratch_shapes=[
            pltpu.VMEM((vocab, LANES), jnp.float32),
            pltpu.VMEM((groups, total + 8, LANES), jnp.float32),
        ],
        compiler_params=pltpu.CompilerParams(vmem_limit_bytes=48 * MIB),
        name="lookup",
    )(ids, counts, table_t)


def cache_kernel(shards, lengths, *refs):
    pieces, (keys, values) = refs[: 2 * shards], refs[2 * shards :]
    layers, positions, width = pieces[0].shape
    pair = 2 * width // HEADS
    limit = lengths[lax.axis_index("table")]
    shard = lax.axis_index("seq")
    lane = lax.broadcasted_iota(jnp.int32, (positions, pair), 1)
    row = lax.broadcasted_iota(jnp.int32, (positions, pair), 0)
    for kind, (target, scale) in enumerate(((keys, 0.5 * (width // HEADS) ** -0.5), (values, 1.0))):
        for index in range(shards):
            kept = row < limit - (shard ^ index) * positions
            for layer in range(layers):
                for head in range(HEADS):
                    mine = (lane // (pair // 2)) == (head % 2)
                    piece = pieces[kind * shards + index][layer, :, pl.ds(head // 2 * pair, pair)]
                    piece = jnp.where(kept & mine, piece.astype(jnp.float32) * scale, 0.0)
                    target[layer, head, pl.ds(index * positions, positions), :] = piece.astype(
                        jnp.bfloat16
                    )


def spread_cache(history, lengths):
    shards = lax.axis_size("seq")
    bits = [1 << k for k in range(shards.bit_length() - 1)]
    kinds = []
    for kind in range(2):
        held = {0: history[0, :, kind]}
        for bit in bits if kind == 0 else bits[::-1]:
            route = [(i, i ^ bit) for i in range(shards)]
            held.update({k ^ bit: lax.ppermute(v, "seq", route) for k, v in list(held.items())})
        kinds.append(held)
    pieces = [kinds[kind][index] for kind in range(2) for index in range(shards)]
    layers, positions, width = pieces[0].shape
    shape = jax.ShapeDtypeStruct(
        (layers, HEADS, positions * shards, 2 * width // HEADS), jnp.bfloat16
    )
    return pl.pallas_call(
        functools.partial(cache_kernel, shards),
        out_shape=(shape, shape),
        in_specs=[SMEM] + [VMEM] * len(pieces),
        out_specs=(VMEM, VMEM),
        compiler_params=pltpu.CompilerParams(vmem_limit_bytes=32 * MIB),
        name="cache",
    )(lengths, *pieces)


def half_silu(half):
    return half + half * jnp.tanh(half)


def normalized(values):
    mean = jnp.mean(values, axis=-1, keepdims=True)
    centred = values - mean
    variance = jnp.mean(centred * centred, axis=-1, keepdims=True)
    return centred * lax.rsqrt(variance + 1e-06)


def dot(left, right):
    return jnp.dot(left, right, preferred_element_type=jnp.float32)


def dot_rows(left, right):
    return lax.dot_general(
        left, right, (((1,), (1,)), ((), ())), preferred_element_type=jnp.float32
    )


def rank_kernel(geometry, counts, pieces, keys, values, w_in, w_out, w_proj, w_back, out, ranked):
    groups, capacity, packing, tile = geometry
    width = w_in.shape[0]
    columns = LANES // packing
    table_index = lax.axis_index("table")
    shard = lax.axis_index("seq")
    step = pl.program_id(0)
    part = tile // packing
    filled = lax.fori_loop(
        0, groups, lambda t, n: n + counts[t, shard, table_index], jnp.int32(0)
    )

    @pl.when(step * tile < filled)
    def _():
        lane = lax.broadcasted_iota(jnp.int32, (part, LANES), 1) // columns
        row = lax.broadcasted_iota(jnp.int32, (part, LANES), 0)
        rows = []
        for piece in range(packing):
            keep = row + (step * tile + piece * part) < filled
            blocks = []
            for block in range(width // LANES):
                value = None
                for spot in range(packing):
                    source = pieces[block * packing + spot].astype(jnp.float32)
                    turn = (spot - piece) % packing * columns
                    if turn:
                        source = pltpu.roll(source, turn, 1)
                    value = source if value is None else jnp.where(lane == spot, source, value)
                blocks.append(jnp.where(keep, value, 0.0))
            rows.append(jnp.concatenate(blocks, axis=1))
        embedded = jnp.concatenate(rows, axis=0)
        embedded16 = embedded.astype(jnp.bfloat16)
        total = embedded
        chunk = 512
        for at in range(0, w_in.shape[1], chunk):
            half = dot(embedded16, w_in[:, at : at + chunk]) * 0.5
            hidden = half_silu(half).astype(jnp.bfloat16)
            total = total + dot(hidden, w_out[at : at + chunk, :])
        states = total.astype(jnp.bfloat16)
        pair = keys.shape[3]
        for layer in range(w_proj.shape[0]):
            normed = normalized(states.astype(jnp.float32)).astype(jnp.bfloat16)
            gate = half_silu(dot(normed, w_proj[layer, :, :width]) * 0.5)
            queries = half_silu(dot(normed, w_proj[layer, :, width:]) * 0.5).astype(jnp.bfloat16)
            attended = []
            for block in range(HEADS // 2):
                query = queries[:, block * pair : (block + 1) * pair]
                got = None
                for head in (2 * block, 2 * block + 1):
                    weights = half_silu(dot_rows(query, keys[layer, head])).astype(jnp.bfloat16)
                    term = dot(weights, values[layer, head])
                    got = term if got is None else got + term
                attended.append(got)
            attended = jnp.concatenate(attended, axis=1)
            mixed = (normalized(attended) * gate).astype(jnp.bfloat16)
            states = (states.astype(jnp.float32) + dot(mixed, w_back[layer])).astype(jnp.bfloat16)
        for block in range(width // LANES):
            ranked[block, pl.ds(pl.multiple_of(step * tile, tile), tile), :] = states[
                :, block * LANES : (block + 1) * LANES
            ].astype(jnp.float32)

    @pl.when(step == pl.num_programs(0) - 1)
    def _():
        row = lax.broadcasted_iota(jnp.int32, (capacity, LANES), 0)

        def slot_block(sender, start):
            amount = counts[sender, shard, table_index]
            for block in range(width // LANES):
                value = ranked[block, pl.ds(start, capacity), :]
                out[
                    pl.ds(pl.multiple_of(sender * capacity, capacity), capacity),
                    block * LANES : (block + 1) * LANES,
                ] = jnp.where(row < amount, value, 0.0).astype(jnp.bfloat16)
            return start + amount

        lax.fori_loop(0, groups, slot_block, jnp.int32(0))


def rank(counts, pieces, keys, values, w_in, w_out, w_proj, w_back, capacity, packing, tile):
    groups, packed_rows, _ = pieces.shape
    total = groups * capacity
    width = w_in.shape[0]
    return pl.pallas_call(
        functools.partial(rank_kernel, (groups, capacity, packing, tile)),
        grid=(total // tile,),
        out_shape=jax.ShapeDtypeStruct((total, width), jnp.bfloat16),
        in_specs=[
            SMEM,
            pl.BlockSpec((groups, tile // packing, LANES), lambda i: (0, i, 0)),
            VMEM, VMEM, VMEM, VMEM, VMEM, VMEM,
        ],
        out_specs=pl.BlockSpec((total, width), lambda i: (0, 0)),
        scratch_shapes=[pltpu.VMEM((width // LANES, total + capacity, LANES), jnp.float32)],
        compiler_params=pltpu.CompilerParams(vmem_limit_bytes=56 * MIB),
        name="rank",
    )(counts, pieces, keys, values, w_in, w_out, w_proj, w_back)


def local(item_ids, item_table, group_counts, lengths, history, w_in, w_out, w_proj, w_back):
    groups = lax.axis_size("table")
    row_count = item_ids.shape[0] // groups
    capacity = 3 * row_count // (2 * groups)
    packing = LANES // item_table.shape[1]
    tile = 256
    total = groups * capacity
    keys, values = spread_cache(history, lengths)
    pieces = lookup(item_ids, group_counts, item_table.T, groups, total, packing, tile)
    pieces = lax.all_to_all(pieces, "table", split_axis=0, concat_axis=0, tiled=True)
    return rank(
        group_counts, pieces, keys, values, w_in, w_out, w_proj, w_back, capacity, packing, tile
    )


def solution(mesh):
    placed = (
        P("seq"),
        P("seq", "table"),
        P(),
        P(),
        P("table", None, None, "seq", None),
        P(),
        P(),
        P(),
        P(),
    )
    return jax.shard_map(
        local, mesh=mesh, in_specs=placed, out_specs=P(("table", "seq"), None), check_vma=False
    )
```

```python
import functools

import jax
import jax.numpy as jnp
from jax import lax
from jax.experimental import pallas as pl
from jax.experimental.pallas import tpu as pltpu
from jax.sharding import PartitionSpec as P

HEADS = 8
LANES = 128
UNROLL = 32
MIB = 1 << 20
ANY = pl.BlockSpec(memory_space=pl.ANY)
SMEM = pl.BlockSpec(memory_space=pltpu.SMEM)
VMEM = pl.BlockSpec(memory_space=pltpu.VMEM)


def lookup_kernel(
    geometry, ids, counts, table_t, out, table, rows_major, picked, id_vector, local_ids, held, sems
):
    low, high = geometry
    columns, vocab = table_t.shape
    groups = counts.shape[0]
    id_count = ids.shape[0]
    row_count = id_count // groups
    packing = LANES // columns
    shard = lax.axis_index("seq")
    get_ids = pltpu.make_async_copy(ids, id_vector, sems.at[0])
    get_ids.start()
    get_counts = pltpu.make_async_copy(counts, held, sems.at[1])
    get_counts.start()
    cuts = 8
    block = vocab // cuts
    get_table = [
        pltpu.make_async_copy(
            table_t.at[:, pl.ds(cut * block, block)],
            table.at[:, pl.ds(cut * block, block)],
            sems.at[3 + cut],
        )
        for cut in range(cuts)
    ]
    for copy in get_table:
        copy.start()
    get_ids.wait()
    id_vector[...] = id_vector[...] - shard * vocab
    put_ids = pltpu.make_async_copy(id_vector, local_ids.at[pl.ds(0, id_count)], sems.at[2])
    put_ids.start()
    for k in range(UNROLL):
        local_ids[id_count + k] = 0
    inner = 1024
    for cut in range(cuts):
        get_table[cut].wait()

        def turn(step, carry, cut=cut):
            at = pl.multiple_of(cut * block + step * inner, inner)
            piece = table[:, pl.ds(at, inner)]
            piece = jnp.concatenate([piece] * packing, axis=0)
            rows_major[pl.ds(at, inner), :] = piece.T.astype(jnp.float32)
            return carry

        lax.fori_loop(0, block // inner, turn, 0)
    get_counts.wait()
    put_ids.wait()

    def sender(sender_id, starts):
        source = sender_id * row_count
        new_starts = []
        for group in range(groups):
            amount = held[sender_id, shard, group]
            start = starts[group]
            first = jnp.maximum(start, low)
            wanted = jnp.minimum(start + amount, high) - first
            from_id = source + (first - start)
            target = first - low

            def several(size):
                def body(step, carry):
                    found = [
                        rows_major[pl.ds(local_ids[from_id + step * size + k], 1), :]
                        for k in range(size)
                    ]
                    for k in range(size):
                        picked[group, pl.ds(target + step * size + k, 1), :] = found[k]
                    return carry

                return body

            wanted = jnp.maximum(wanted, 0)
            rounds = wanted // UNROLL
            lax.fori_loop(0, rounds, several(UNROLL), 0)
            lax.fori_loop(rounds * (UNROLL // 8), (wanted + 7) // 8, several(8), 0)
            source = source + amount
            new_starts.append(start + amount)
        return tuple(new_starts)

    lax.fori_loop(0, groups, sender, (jnp.int32(0),) * groups)

    part = out.shape[1]
    lane = lax.broadcasted_iota(jnp.int32, (part, LANES), 1) // columns

    def pack(group, carry):
        value = picked[group, pl.ds(0, part), :]
        for piece in range(1, packing):
            value = jnp.where(lane == piece, picked[group, pl.ds(piece * part, part), :], value)
        out[group] = value.astype(jnp.bfloat16)
        return carry

    lax.fori_loop(0, groups, pack, 0)


def lookup(ids, counts, table_t, low, high):
    columns, vocab = table_t.shape
    packing = LANES // columns
    groups = counts.shape[0]
    return pl.pallas_call(
        functools.partial(lookup_kernel, (low, high)),
        out_shape=jax.ShapeDtypeStruct((groups, (high - low) // packing, LANES), jnp.bfloat16),
        in_specs=[ANY, ANY, ANY],
        out_specs=VMEM,
        scratch_shapes=[
            pltpu.VMEM((columns, vocab), jnp.bfloat16),
            pltpu.VMEM((vocab, LANES), jnp.float32),
            pltpu.VMEM((groups, high - low + UNROLL, LANES), jnp.float32),
            pltpu.VMEM(ids.shape, jnp.int32),
            pltpu.SMEM((ids.shape[0] + UNROLL,), jnp.int32),
            pltpu.SMEM(counts.shape, jnp.int32),
            pltpu.SemaphoreType.DMA((11,)),
        ],
        compiler_params=pltpu.CompilerParams(vmem_limit_bytes=62 * MIB),
        cost_estimate=pl.CostEstimate(
            flops=20_000_000_000, bytes_accessed=40_000_000, transcendentals=0
        ),
        name="lookup",
    )(ids, counts, table_t)


def cache_kernel(shards, lengths, *refs):
    pieces, (keys, values) = refs[: 2 * shards], refs[2 * shards :]
    layers, piece_rows, width = pieces[0].shape
    positions = shards * piece_rows
    pair = 2 * width // HEADS
    shard = lax.axis_index("seq")
    limit = lengths[lax.axis_index("table")]
    lane = lax.broadcasted_iota(jnp.int32, (positions, pair), 1)
    row = lax.broadcasted_iota(jnp.int32, (piece_rows, pair), 0)
    place = jnp.concatenate([row + (shard ^ k) * piece_rows for k in range(shards)], axis=0)
    kept = place < limit
    scale = 0.5 * (width // HEADS) ** -0.5
    for layer in range(layers):
        for block in range(HEADS // 2):
            columns = pl.ds(block * pair, pair)
            for kind in range(2):
                whole = jnp.concatenate(
                    [pieces[kind * shards + k][layer, :, columns] for k in range(shards)], axis=0
                ).astype(jnp.float32)
                for half in range(2):
                    mine = kept & ((lane // (pair // 2)) == half)
                    spot = pl.ds(half * positions, positions)
                    if kind == 0:
                        value = jnp.where(mine, whole * scale, 0.0).astype(jnp.bfloat16)
                        keys[layer, block, :, spot] = value.T
                    else:
                        value = jnp.where(mine, whole, 0.0).astype(jnp.bfloat16)
                        values[layer, block, spot, :] = value


def spread_cache(history, lengths):
    shards = lax.axis_size("seq")
    bits = [1 << k for k in range(shards.bit_length() - 1)]
    kinds = []
    for kind in range(2):
        held = {0: history[0, :, kind]}
        for bit in bits if kind == 0 else bits[::-1]:
            route = [(i, i ^ bit) for i in range(shards)]
            held.update({k ^ bit: lax.ppermute(v, "seq", route) for k, v in list(held.items())})
        kinds.append(held)
    pieces = [kinds[kind][index] for kind in range(2) for index in range(shards)]
    layers, piece_rows, width = pieces[0].shape
    pair, positions = 2 * width // HEADS, 2 * piece_rows * shards
    return pl.pallas_call(
        functools.partial(cache_kernel, shards),
        out_shape=(
            jax.ShapeDtypeStruct((layers, HEADS // 2, pair, positions), jnp.bfloat16),
            jax.ShapeDtypeStruct((layers, HEADS // 2, positions, pair), jnp.bfloat16),
        ),
        in_specs=[SMEM] + [VMEM] * len(pieces),
        out_specs=(VMEM, VMEM),
        compiler_params=pltpu.CompilerParams(vmem_limit_bytes=32 * MIB),
        name="cache",
    )(lengths, *pieces)


def half_silu(half):
    return half + half * jnp.tanh(half)


def dot(left, right):
    return jnp.dot(left, right, preferred_element_type=jnp.float32)


def row_mean(values):
    width = values.shape[1]
    partial = sum(values[:, at : at + LANES] for at in range(0, width, LANES))
    high = partial.astype(jnp.bfloat16)
    low = (partial - high.astype(jnp.float32)).astype(jnp.bfloat16)
    ones = jnp.full((2 * LANES, LANES), 1.0 / width, jnp.bfloat16)
    mean = dot(jnp.concatenate([high, low], axis=1), ones)
    return jnp.concatenate([mean] * (width // LANES), axis=1)


def normalized(values):
    centred = values - row_mean(values)
    return centred * lax.rsqrt(row_mean(centred * centred) + 1e-06)


def rank_kernel(low, capacity, done, counts, pieces, *refs):
    before, refs = refs[:done], refs[done:]
    sources, out, refs = refs[:6], refs[6], refs[7:]
    ranked, refs = (refs[0], refs[1:]) if done else (None, refs)
    held, sems = refs[:6], refs[6]
    keys, values, w_in, w_out, w_proj, w_back = held
    groups, part, _ = pieces.shape
    width = w_in.shape[0]
    packing = groups * LANES // width
    columns = LANES // packing
    tile = part * packing
    table_index = lax.axis_index("table")
    shard = lax.axis_index("seq")
    filled = lax.fori_loop(
        0, groups, lambda t, n: n + counts[t, shard, table_index], jnp.int32(0)
    )

    def keep(states):
        if done:
            for block in range(width // LANES):
                ranked[block, pl.ds(low, tile), :] = states[
                    :, block * LANES : (block + 1) * LANES
                ].astype(jnp.float32)
        else:
            out[...] = states

    if done:
        at = 0
        for piece in before:
            for block in range(width // LANES):
                ranked[block, pl.ds(at, piece.shape[0]), :] = piece[
                    :, pl.ds(block * LANES, LANES)
                ].astype(jnp.float32)
            at += piece.shape[0]

    @pl.when(low < filled)
    def _():
        copies = [
            pltpu.make_async_copy(sources[k], held[k], sems.at[k]) for k in (2, 3, 4, 0, 1, 5)
        ]
        for copy in copies:
            copy.start()
        lane = lax.broadcasted_iota(jnp.int32, (part, LANES), 1) // columns
        row = lax.broadcasted_iota(jnp.int32, (part, LANES), 0)
        rows = []
        for piece in range(packing):
            wanted = row + (low + piece * part) < filled
            blocks = []
            for block in range(width // LANES):
                value = None
                for spot in range(packing):
                    source = pieces[block * packing + spot].astype(jnp.float32)
                    turn = (spot - piece) % packing * columns
                    if turn:
                        source = pltpu.roll(source, turn, 1)
                    value = source if value is None else jnp.where(lane == spot, source, value)
                blocks.append(jnp.where(wanted, value, 0.0))
            rows.append(jnp.concatenate(blocks, axis=1))
        embedded = jnp.concatenate(rows, axis=0)
        embedded16 = embedded.astype(jnp.bfloat16)
        total = embedded
        chunk = width
        for copy in copies[:2]:
            copy.wait()
        for at in range(0, w_in.shape[1], chunk):
            half = dot(embedded16, w_in[:, at : at + chunk]) * 0.5
            hidden = half_silu(half).astype(jnp.bfloat16)
            total = total + dot(hidden, w_out[at : at + chunk, :])
        states = total.astype(jnp.bfloat16)
        pair = keys.shape[2]
        for copy in copies[2:]:
            copy.wait()
        for layer in range(w_proj.shape[0]):
            normed = normalized(states.astype(jnp.float32)).astype(jnp.bfloat16)
            gate = half_silu(dot(normed, w_proj[layer, :, :width]) * 0.5)
            queries = half_silu(dot(normed, w_proj[layer, :, width:]) * 0.5).astype(jnp.bfloat16)
            attended = []
            for block in range(HEADS // 2):
                query = queries[:, block * pair : (block + 1) * pair]
                weights = half_silu(dot(query, keys[layer, block])).astype(jnp.bfloat16)
                attended.append(dot(weights, values[layer, block]))
            attended = jnp.concatenate(attended, axis=1)
            mixed = (normalized(attended) * gate).astype(jnp.bfloat16)
            states = (states.astype(jnp.float32) + dot(mixed, w_back[layer])).astype(jnp.bfloat16)
        keep(states)

    if done:
        row = lax.broadcasted_iota(jnp.int32, (capacity, LANES), 0)

        def slot_block(sender, start):
            amount = counts[sender, shard, table_index]
            for block in range(width // LANES):
                value = ranked[block, pl.ds(start, capacity), :]
                out[
                    pl.ds(pl.multiple_of(sender * capacity, capacity), capacity),
                    block * LANES : (block + 1) * LANES,
                ] = jnp.where(row < amount, value, 0.0).astype(jnp.bfloat16)
            return start + amount

        lax.fori_loop(0, groups, slot_block, jnp.int32(0))


def rank(counts, pieces, before, sources, low, capacity):
    groups, part, _ = pieces.shape
    width = sources[2].shape[0]
    tile = part * groups * LANES // width
    total = groups * capacity
    done = len(before)
    scratch = [pltpu.VMEM(source.shape, source.dtype) for source in sources]
    if done:
        scratch = [pltpu.VMEM((width // LANES, total + capacity, LANES), jnp.float32)] + scratch
    return pl.pallas_call(
        functools.partial(rank_kernel, low, capacity, done),
        out_shape=jax.ShapeDtypeStruct((total if done else tile, width), jnp.bfloat16),
        in_specs=[SMEM, VMEM] + [VMEM] * done + [ANY] * len(sources),
        out_specs=VMEM,
        scratch_shapes=scratch + [pltpu.SemaphoreType.DMA((len(sources),))],
        compiler_params=pltpu.CompilerParams(vmem_limit_bytes=62 * MIB),
        cost_estimate=pl.CostEstimate(
            flops=20_000_000_000, bytes_accessed=20_000_000, transcendentals=0
        ),
        name="rank",
    )(counts, pieces, *before, *sources)


def local(item_ids, item_table, group_counts, lengths, history, w_in, w_out, w_proj, w_back):
    groups = lax.axis_size("table")
    row_count = item_ids.shape[0] // groups
    capacity = 3 * row_count // (2 * groups)
    total = groups * capacity
    cuts = (0, total * 7 // 12, total)
    table_t = item_table.T
    pieces = []
    for low, high in zip(cuts, cuts[1:]):
        found = lookup(item_ids, group_counts, table_t, low, high)
        pieces.append(lax.all_to_all(found, "table", split_axis=0, concat_axis=0, tiled=True))
    keys, values = spread_cache(history, lengths)
    sources = (keys, values, w_in, w_out, w_proj, w_back)
    states = []
    for part, low in enumerate(cuts[:-1]):
        before = states if part == len(cuts) - 2 else []
        states = states + [rank(group_counts, pieces[part], before, sources, low, capacity)]
    return states[-1]


def solution(mesh):
    placed = (
        P("seq"),
        P("seq", "table"),
        P(),
        P(),
        P("table", None, None, "seq", None),
        P(),
        P(),
        P(),
        P(),
    )
    return jax.shard_map(
        local, mesh=mesh, in_specs=placed, out_specs=P(("table", "seq"), None), check_vma=False
    )
```

```python
import functools

import jax
import jax.numpy as jnp
from jax import lax
from jax.experimental import pallas as pl
from jax.experimental.pallas import tpu as pltpu
from jax.sharding import PartitionSpec as P

HEADS = 8
LANES = 128
UNROLL = 64
MIB = 1 << 20
ANY = pl.BlockSpec(memory_space=pl.ANY)
SMEM = pl.BlockSpec(memory_space=pltpu.SMEM)
VMEM = pl.BlockSpec(memory_space=pltpu.VMEM)


def lookup_kernel(cuts, ids, counts, table_t, *refs):
    outs, refs = refs[: len(cuts) - 1], refs[len(cuts) - 1 :]
    table, rows_major, found, picked, id_vector, local_ids, held, sems = refs
    columns, vocab = table_t.shape
    groups = counts.shape[0]
    id_count = ids.shape[0]
    row_count = id_count // groups
    packing = LANES // columns
    capacity = cuts[-1] // groups
    shard = lax.axis_index("seq")
    get_ids = pltpu.make_async_copy(ids, id_vector, sems.at[0])
    get_ids.start()
    get_counts = pltpu.make_async_copy(counts, held, sems.at[1])
    get_counts.start()
    parts = 8
    block = vocab // parts
    get_table = [
        pltpu.make_async_copy(
            table_t.at[:, pl.ds(part * block, block)],
            table.at[:, pl.ds(part * block, block)],
            sems.at[3 + part],
        )
        for part in range(parts)
    ]
    for copy in get_table:
        copy.start()
    get_ids.wait()
    id_vector[...] = id_vector[...] - shard * vocab
    put_ids = pltpu.make_async_copy(id_vector, local_ids, sems.at[2])
    put_ids.start()
    inner = 1024
    for part in range(parts):
        get_table[part].wait()

        def turn(step, carry, part=part):
            at = pl.multiple_of(part * block + step * inner, inner)
            piece = table[:, pl.ds(at, inner)]
            piece = jnp.concatenate([piece] * packing, axis=0)
            rows_major[pl.ds(at, inner), :] = piece.T.astype(jnp.float32)
            return carry

        lax.fori_loop(0, block // inner, turn, 0)
    get_counts.wait()
    put_ids.wait()

    def gather(step, carry):
        at = pl.multiple_of(step * UNROLL, UNROLL)
        rows = [rows_major[pl.ds(local_ids[at + k], 1), :] for k in range(UNROLL)]
        for k in range(UNROLL):
            found[pl.ds(at + k, 1), :] = rows[k]
        return carry

    lax.fori_loop(0, id_count // UNROLL, gather, 0)

    def sender(sender_id, starts):
        source = sender_id * row_count
        new_starts = []
        for group in range(groups):
            amount = held[sender_id, shard, group]
            picked[group, pl.ds(starts[group], capacity), :] = found[pl.ds(source, capacity), :]
            source = source + amount
            new_starts.append(starts[group] + amount)
        return tuple(new_starts)

    lax.fori_loop(0, groups, sender, (jnp.int32(0),) * groups)

    def pack(group, carry):
        for low, out in zip(cuts, outs):
            part = out.shape[1]
            lane = lax.broadcasted_iota(jnp.int32, (part, LANES), 1) // columns
            value = picked[group, pl.ds(low, part), :]
            for piece in range(1, packing):
                more = picked[group, pl.ds(low + piece * part, part), :]
                value = jnp.where(lane == piece, more, value)
            out[group] = value.astype(jnp.bfloat16)
        return carry

    lax.fori_loop(0, groups, pack, 0)


def lookup(ids, counts, table_t, cuts):
    columns, vocab = table_t.shape
    packing = LANES // columns
    groups = counts.shape[0]
    total = cuts[-1]
    return pl.pallas_call(
        functools.partial(lookup_kernel, cuts),
        out_shape=tuple(
            jax.ShapeDtypeStruct((groups, (high - low) // packing, LANES), jnp.bfloat16)
            for low, high in zip(cuts, cuts[1:])
        ),
        in_specs=[ANY, ANY, ANY],
        out_specs=(VMEM,) * (len(cuts) - 1),
        scratch_shapes=[
            pltpu.VMEM((columns, vocab), jnp.bfloat16),
            pltpu.VMEM((vocab, LANES), jnp.float32),
            pltpu.VMEM((ids.shape[0] + total // groups, LANES), jnp.float32),
            pltpu.VMEM((groups, total + total // groups, LANES), jnp.float32),
            pltpu.VMEM(ids.shape, jnp.int32),
            pltpu.SMEM(ids.shape, jnp.int32),
            pltpu.SMEM(counts.shape, jnp.int32),
            pltpu.SemaphoreType.DMA((11,)),
        ],
        compiler_params=pltpu.CompilerParams(vmem_limit_bytes=62 * MIB),
        name="lookup",
    )(ids, counts, table_t)


def gather_history(history):
    shards = lax.axis_size("seq")
    bits = [1 << k for k in range(shards.bit_length() - 1)]
    pieces = []
    for kind in range(2):
        held = {0: history[0, :, kind]}
        for bit in bits if kind == 0 else bits[::-1]:
            route = [(i, i ^ bit) for i in range(shards)]
            held.update({k ^ bit: lax.ppermute(v, "seq", route) for k, v in list(held.items())})
        pieces += [held[index] for index in range(shards)]
    return pieces


def half_silu(half):
    return half + half * jnp.tanh(half)


def dot(left, right):
    return jnp.dot(left, right, preferred_element_type=jnp.float32)


def dot_rows(left, right):
    return lax.dot_general(
        left, right, (((1,), (1,)), ((), ())), preferred_element_type=jnp.float32
    )


def row_mean(values):
    width = values.shape[1]
    partial = sum(values[:, at : at + LANES] for at in range(0, width, LANES))
    high = partial.astype(jnp.bfloat16)
    low = (partial - high.astype(jnp.float32)).astype(jnp.bfloat16)
    ones = jnp.full((2 * LANES, LANES), 1.0 / width, jnp.bfloat16)
    mean = dot(jnp.concatenate([high, low], axis=1), ones)
    return jnp.concatenate([mean] * (width // LANES), axis=1)


def normalized(values):
    centred = values - row_mean(values)
    return centred * lax.rsqrt(row_mean(centred * centred) + 1e-06)


def rank_kernel(low, capacity, done, shards, counts, lengths, pieces, *refs):
    before, refs = refs[:done], refs[done:]
    history, refs = refs[: 2 * shards], refs[2 * shards :]
    weights, out, refs = refs[:4], refs[4], refs[5:]
    ranked, refs = (refs[0], refs[1:]) if done else (None, refs)
    keys, values, w_in, w_out, w_proj, w_back, sems = refs
    groups, part, _ = pieces.shape
    width = w_in.shape[0]
    packing = groups * LANES // width
    columns = LANES // packing
    tile = part * packing
    table_index = lax.axis_index("table")
    shard = lax.axis_index("seq")
    filled = lax.fori_loop(
        0, groups, lambda t, n: n + counts[t, shard, table_index], jnp.int32(0)
    )

    def keep(states):
        if done:
            for block in range(width // LANES):
                ranked[block, pl.ds(low, tile), :] = states[
                    :, block * LANES : (block + 1) * LANES
                ].astype(jnp.float32)
        else:
            out[...] = states

    if done:
        at = 0
        for piece in before:
            for block in range(width // LANES):
                ranked[block, pl.ds(at, piece.shape[0]), :] = piece[
                    :, pl.ds(block * LANES, LANES)
                ].astype(jnp.float32)
            at += piece.shape[0]

    @pl.when(low < filled)
    def _():
        chunk = width
        head, tail = pl.ds(0, chunk), pl.ds(chunk, w_in.shape[1] - chunk)
        views = [
            (weights[0].at[:, head], w_in.at[:, head]),
            (weights[1].at[head], w_out.at[head]),
            (weights[0].at[:, tail], w_in.at[:, tail]),
            (weights[1].at[tail], w_out.at[tail]),
            (weights[2], w_proj),
            (weights[3], w_back),
        ]
        piece_rows = keys.shape[1] // shards
        for k in range(2 * shards):
            place = pl.multiple_of((shard ^ (k % shards)) * piece_rows, piece_rows)
            target = (keys, values)[k // shards]
            views.append((history[k], target.at[:, pl.ds(place, piece_rows), :]))
        copies = [
            pltpu.make_async_copy(source, target, sems.at[k])
            for k, (source, target) in enumerate(views)
        ]
        for copy in copies[:4]:
            copy.start()
        lane = lax.broadcasted_iota(jnp.int32, (part, LANES), 1) // columns
        row = lax.broadcasted_iota(jnp.int32, (part, LANES), 0)
        rows = []
        for piece in range(packing):
            wanted = row + (low + piece * part) < filled
            blocks = []
            for block in range(width // LANES):
                value = None
                for spot in range(packing):
                    source = pieces[block * packing + spot].astype(jnp.float32)
                    turn = (spot - piece) % packing * columns
                    if turn:
                        source = pltpu.roll(source, turn, 1)
                    value = source if value is None else jnp.where(lane == spot, source, value)
                blocks.append(jnp.where(wanted, value, 0.0))
            rows.append(jnp.concatenate(blocks, axis=1))
        embedded = jnp.concatenate(rows, axis=0)
        embedded16 = embedded.astype(jnp.bfloat16)
        total = embedded
        for copy in copies[:2]:
            copy.wait()
        for copy in copies[4:]:
            copy.start()
        for at in range(0, w_in.shape[1], chunk):
            if at == chunk:
                for copy in copies[2:4]:
                    copy.wait()
            half = dot(embedded16, w_in[:, at : at + chunk]) * 0.5
            hidden = half_silu(half).astype(jnp.bfloat16)
            total = total + dot(hidden, w_out[at : at + chunk, :])
        states = total.astype(jnp.bfloat16)
        for copy in copies[4:]:
            copy.wait()
        pair = 2 * width // HEADS
        limit = lengths[table_index]
        cached = lax.broadcasted_iota(jnp.int32, keys.shape[1:], 0) < limit
        first = lax.broadcasted_iota(jnp.int32, (tile, pair), 1) < pair // 2
        scale = 0.5 * (width // HEADS) ** -0.5
        for layer in range(w_proj.shape[0]):
            normed = normalized(states.astype(jnp.float32)).astype(jnp.bfloat16)
            queries = half_silu(dot(normed, w_proj[layer, :, width:]) * 0.5) * scale
            queries = queries.astype(jnp.bfloat16)
            kept = jnp.where(cached, keys[layer], jnp.zeros((), jnp.bfloat16))

            def score(block):
                query = queries[:, block * pair : (block + 1) * pair]
                none = jnp.zeros((), jnp.bfloat16)
                both = jnp.concatenate(
                    [jnp.where(first, query, none), jnp.where(first, none, query)], axis=0
                )
                return dot_rows(both, kept[:, block * pair : (block + 1) * pair])

            attended = []
            scores = score(0)
            for block in range(HEADS // 2):
                following = score(block + 1) if block + 1 < HEADS // 2 else None
                weighted = half_silu(scores).astype(jnp.bfloat16)
                both = dot(weighted, values[layer, :, block * pair : (block + 1) * pair])
                attended.append(jnp.where(first, both[:tile], both[tile:]))
                scores = following
            attended = jnp.concatenate(attended, axis=1)
            gate = half_silu(dot(normed, w_proj[layer, :, :width]) * 0.5)
            mixed = (normalized(attended) * gate).astype(jnp.bfloat16)
            states = (states.astype(jnp.float32) + dot(mixed, w_back[layer])).astype(jnp.bfloat16)
        keep(states)

    if done:
        row = lax.broadcasted_iota(jnp.int32, (capacity, LANES), 0)

        def slot_block(sender, start):
            amount = counts[sender, shard, table_index]
            for block in range(width // LANES):
                value = ranked[block, pl.ds(start, capacity), :]
                out[
                    pl.ds(pl.multiple_of(sender * capacity, capacity), capacity),
                    block * LANES : (block + 1) * LANES,
                ] = jnp.where(row < amount, value, 0.0).astype(jnp.bfloat16)
            return start + amount

        lax.fori_loop(0, groups, slot_block, jnp.int32(0))


def rank(counts, lengths, pieces, before, history, weights, low, capacity):
    groups, part, _ = pieces.shape
    width = weights[0].shape[0]
    tile = part * groups * LANES // width
    total = groups * capacity
    done = len(before)
    layers, piece_rows, _ = history[0].shape
    shards = len(history) // 2
    scratch = [pltpu.VMEM((layers, shards * piece_rows, width), jnp.bfloat16)] * 2
    scratch += [pltpu.VMEM(weight.shape, weight.dtype) for weight in weights]
    scratch += [pltpu.SemaphoreType.DMA((len(weights) + 2 + len(history),))]
    if done:
        scratch = [pltpu.VMEM((width // LANES, total + capacity, LANES), jnp.float32)] + scratch
    return pl.pallas_call(
        functools.partial(rank_kernel, low, capacity, done, shards),
        out_shape=jax.ShapeDtypeStruct((total if done else tile, width), jnp.bfloat16),
        in_specs=[SMEM, SMEM, VMEM] + [VMEM] * done + [ANY] * (len(history) + len(weights)),
        out_specs=VMEM,
        scratch_shapes=scratch,
        compiler_params=pltpu.CompilerParams(vmem_limit_bytes=62 * MIB),
        cost_estimate=pl.CostEstimate(
            flops=20_000_000_000, bytes_accessed=20_000_000, transcendentals=0
        ),
        name="rank",
    )(counts, lengths, pieces, *before, *history, *weights)


def local(item_ids, item_table, group_counts, lengths, history, w_in, w_out, w_proj, w_back):
    groups = lax.axis_size("table")
    row_count = item_ids.shape[0] // groups
    capacity = 3 * row_count // (2 * groups)
    total = groups * capacity
    cuts = (0, total * 13 // 24, total)
    table_t = item_table.T
    found = lookup(item_ids, group_counts, table_t, cuts)
    pieces = [
        lax.all_to_all(chunk, "table", split_axis=0, concat_axis=0, tiled=True) for chunk in found
    ]
    history = gather_history(history)
    weights = (w_in, w_out, w_proj, w_back)
    states = []
    for low, chunk in zip(cuts, pieces):
        before = states if low == cuts[-2] else []
        states = states + [
            rank(group_counts, lengths, chunk, before, history, weights, low, capacity)
        ]
    return states[-1]


def solution(mesh):
    placed = (
        P("seq"),
        P("seq", "table"),
        P(),
        P(),
        P("table", None, None, "seq", None),
        P(),
        P(),
        P(),
        P(),
    )
    return jax.shard_map(
        local, mesh=mesh, in_specs=placed, out_specs=P(("table", "seq"), None), check_vma=False
    )
```

```python
import functools

import jax
import jax.numpy as jnp
from jax import lax
from jax.experimental import pallas as pl
from jax.experimental.pallas import tpu as pltpu
from jax.sharding import PartitionSpec as P

HEADS = 8
LANES = 128
UNROLL = 256
MIB = 1 << 20
ANY = pl.BlockSpec(memory_space=pl.ANY)
SMEM = pl.BlockSpec(memory_space=pltpu.SMEM)
VMEM = pl.BlockSpec(memory_space=pltpu.VMEM)


def lookup_kernel(cuts, ids, counts, table_t, *refs):
    outs, refs = refs[: len(cuts) - 1], refs[len(cuts) - 1 :]
    table, rows_major, found, picked, id_vector, local_ids, held, sems = refs
    columns, vocab = table_t.shape
    groups = counts.shape[0]
    id_count = ids.shape[0]
    row_count = id_count // groups
    packing = LANES // columns
    capacity = cuts[-1] // groups
    shard = lax.axis_index("seq")
    get_ids = pltpu.make_async_copy(ids, id_vector, sems.at[0])
    get_ids.start()
    get_counts = pltpu.make_async_copy(counts, held, sems.at[1])
    get_counts.start()
    parts = 8
    block = vocab // parts
    get_table = [
        pltpu.make_async_copy(
            table_t.at[:, pl.ds(part * block, block)],
            table.at[:, pl.ds(part * block, block)],
            sems.at[3 + part],
        )
        for part in range(parts)
    ]
    for copy in get_table:
        copy.start()
    get_ids.wait()
    id_vector[...] = id_vector[...] - shard * vocab
    put_ids = pltpu.make_async_copy(id_vector, local_ids, sems.at[2])
    put_ids.start()
    for part in range(parts):
        get_table[part].wait()
        piece = table[:, part * block : (part + 1) * block]
        piece = jnp.concatenate([piece] * packing, axis=0)
        rows_major[pl.ds(part * block, block), :] = piece.T.astype(jnp.float32)
    get_counts.wait()
    put_ids.wait()

    def gather(step, carry):
        at = pl.multiple_of(step * UNROLL, UNROLL)
        rows = [rows_major[pl.ds(local_ids[at + k], 1), :] for k in range(UNROLL)]
        for k in range(UNROLL):
            found[pl.ds(at + k, 1), :] = rows[k]
        return carry

    lax.fori_loop(0, id_count // UNROLL, gather, 0)

    def sender(sender_id, starts):
        source = sender_id * row_count
        new_starts = []
        for group in range(groups):
            amount = held[sender_id, shard, group]
            picked[group, pl.ds(starts[group], capacity), :] = found[pl.ds(source, capacity), :]
            source = source + amount
            new_starts.append(starts[group] + amount)
        return tuple(new_starts)

    lax.fori_loop(0, groups, sender, (jnp.int32(0),) * groups)

    def pack(group, carry):
        for low, out in zip(cuts, outs):
            part = out.shape[1]
            lane = lax.broadcasted_iota(jnp.int32, (part, LANES), 1) // columns
            value = picked[group, pl.ds(low, part), :]
            for piece in range(1, packing):
                more = picked[group, pl.ds(low + piece * part, part), :]
                value = jnp.where(lane == piece, more, value)
            out[group] = value.astype(jnp.bfloat16)
        return carry

    lax.fori_loop(0, groups, pack, 0)


def lookup(ids, counts, table_t, cuts):
    columns, vocab = table_t.shape
    packing = LANES // columns
    groups = counts.shape[0]
    total = cuts[-1]
    return pl.pallas_call(
        functools.partial(lookup_kernel, cuts),
        out_shape=tuple(
            jax.ShapeDtypeStruct((groups, (high - low) // packing, LANES), jnp.bfloat16)
            for low, high in zip(cuts, cuts[1:])
        ),
        in_specs=[ANY, ANY, ANY],
        out_specs=(VMEM,) * (len(cuts) - 1),
        scratch_shapes=[
            pltpu.VMEM((columns, vocab), jnp.bfloat16),
            pltpu.VMEM((vocab, LANES), jnp.float32),
            pltpu.VMEM((ids.shape[0] + total // groups, LANES), jnp.float32),
            pltpu.VMEM((groups, total + total // groups, LANES), jnp.float32),
            pltpu.VMEM(ids.shape, jnp.int32),
            pltpu.SMEM(ids.shape, jnp.int32),
            pltpu.SMEM(counts.shape, jnp.int32),
            pltpu.SemaphoreType.DMA((11,)),
        ],
        compiler_params=pltpu.CompilerParams(vmem_limit_bytes=64 * MIB - MIB // 4),
        name="lookup",
    )(ids, counts, table_t)


def gather_history(history):
    shards = lax.axis_size("seq")
    bits = [1 << k for k in range(shards.bit_length() - 1)]
    pieces = []
    for kind in range(2):
        held = {0: history[0, :, kind]}
        for bit in bits if kind == 0 else bits[::-1]:
            route = [(i, i ^ bit) for i in range(shards)]
            held.update({k ^ bit: lax.ppermute(v, "seq", route) for k, v in list(held.items())})
        pieces += [held[index] for index in range(shards)]
    return pieces


def half_silu(half):
    return half + half * jnp.tanh(half)


def dot(left, right):
    return jnp.dot(left, right, preferred_element_type=jnp.float32)


def dot_rows(left, right):
    return lax.dot_general(
        left, right, (((1,), (1,)), ((), ())), preferred_element_type=jnp.float32
    )


def row_mean(blocks):
    partial = sum(blocks[1:], blocks[0])
    high = partial.astype(jnp.bfloat16)
    low = (partial - high.astype(jnp.float32)).astype(jnp.bfloat16)
    ones = jnp.full((2 * LANES, LANES), 1.0 / (LANES * len(blocks)), jnp.bfloat16)
    return dot(jnp.concatenate([high, low], axis=1), ones)


def normalized(blocks):
    mean = row_mean(blocks)
    centred = [block - mean for block in blocks]
    factor = lax.rsqrt(row_mean([block * block for block in centred]) + 1e-06)
    return [block * factor for block in centred]


def in_blocks(values):
    return [values[:, at : at + LANES] for at in range(0, values.shape[1], LANES)]


def rank_kernel(low, capacity, done, shards, counts, lengths, pieces, *refs):
    before, refs = refs[:done], refs[done:]
    history, refs = refs[: 2 * shards], refs[2 * shards :]
    weights, out, refs = refs[:4], refs[4], refs[5:]
    ranked, refs = (refs[0], refs[1:]) if done else (None, refs)
    got, keys, values, w_in, w_out, w_proj, w_back, sems, refs = *refs[:8], refs[8:]
    pieces_in_hbm, pieces = pieces, got
    groups, part, _ = pieces.shape
    width = w_in.shape[0]
    packing = groups * LANES // width
    columns = LANES // packing
    tile = part * packing
    table_index = lax.axis_index("table")
    shard = lax.axis_index("seq")
    filled = lax.fori_loop(
        0, groups, lambda t, n: n + counts[t, shard, table_index], jnp.int32(0)
    )

    get_pieces = pltpu.make_async_copy(pieces_in_hbm, pieces, sems.at[sems.shape[0] - 1])
    get_before = []
    for k, piece in enumerate(before):
        get_before.append(pltpu.make_async_copy(piece, refs[k], sems.at[sems.shape[0] - 2 - k]))
        get_before[-1].start()

    def keep(states):
        if done:
            for block in range(width // LANES):
                ranked[block, pl.ds(low, tile), :] = states[
                    :, block * LANES : (block + 1) * LANES
                ].astype(jnp.float32)
        else:
            out[...] = states

    if done:
        slots, put_sems = refs[done], refs[done + 1]
        slot_row = lax.broadcasted_iota(jnp.int32, (capacity, LANES), 0)

    def put(sender):
        place = pl.ds(pl.multiple_of(sender * capacity, capacity), capacity)
        return pltpu.make_async_copy(slots.at[place], out.at[place], put_sems.at[sender])

    def fill_before():
        at = 0
        for copy, piece in zip(get_before, refs):
            copy.wait()
            for block in range(width // LANES):
                ranked[block, pl.ds(at, piece.shape[0]), :] = piece[
                    :, pl.ds(block * LANES, LANES)
                ].astype(jnp.float32)
            at += piece.shape[0]

    def fill_slots(early):
        def slot_block(sender, start):
            amount = counts[sender, shard, table_index]

            @pl.when((start + amount <= low) == early)
            def _():
                for block in range(width // LANES):
                    value = ranked[block, pl.ds(start, capacity), :]
                    slots[
                        pl.ds(pl.multiple_of(sender * capacity, capacity), capacity),
                        block * LANES : (block + 1) * LANES,
                    ] = jnp.where(slot_row < amount, value, 0.0).astype(jnp.bfloat16)
                put(sender).start()

            return start + amount

        lax.fori_loop(0, groups, slot_block, jnp.int32(0))

    @pl.when(low < filled)
    def _():
        chunk = width
        head, tail = pl.ds(0, chunk), pl.ds(chunk, w_in.shape[1] - chunk)
        views = [
            (weights[0].at[:, head], w_in.at[:, head]),
            (weights[1].at[head], w_out.at[head]),
            (weights[0].at[:, tail], w_in.at[:, tail]),
            (weights[1].at[tail], w_out.at[tail]),
            (weights[2], w_proj),
            (weights[3], w_back),
        ]
        piece_rows = keys.shape[1] // shards
        for k in range(2 * shards):
            place = pl.multiple_of((shard ^ (k % shards)) * piece_rows, piece_rows)
            target = (keys, values)[k // shards]
            views.append((history[k], target.at[:, pl.ds(place, piece_rows), :]))
        copies = [
            pltpu.make_async_copy(source, target, sems.at[k])
            for k, (source, target) in enumerate(views)
        ]
        copies[0].start()
        get_pieces.start()
        for copy in copies[1:4]:
            copy.start()
        if done:
            fill_before()
            fill_slots(True)
        get_pieces.wait()
        lane = lax.broadcasted_iota(jnp.int32, (part, LANES), 1) // columns
        row = lax.broadcasted_iota(jnp.int32, (part, LANES), 0)
        rows = []
        for piece in range(packing):
            wanted = row + (low + piece * part) < filled
            blocks = []
            for block in range(width // LANES):
                value = None
                for spot in range(packing):
                    source = pieces[block * packing + spot].astype(jnp.float32)
                    turn = (spot - piece) % packing * columns
                    if turn:
                        source = pltpu.roll(source, turn, 1)
                    value = source if value is None else jnp.where(lane == spot, source, value)
                blocks.append(jnp.where(wanted, value, 0.0))
            rows.append(jnp.concatenate(blocks, axis=1))
        embedded = jnp.concatenate(rows, axis=0)
        embedded16 = embedded.astype(jnp.bfloat16)
        total = embedded
        for copy in copies[:2]:
            copy.wait()
        for copy in copies[4:]:
            copy.start()
        for at in range(0, w_in.shape[1], chunk):
            if at == chunk:
                for copy in copies[2:4]:
                    copy.wait()
            half = dot(embedded16, w_in[:, at : at + chunk]) * 0.5
            hidden = half_silu(half).astype(jnp.bfloat16)
            total = total + dot(hidden, w_out[at : at + chunk, :])
        states = total.astype(jnp.bfloat16)
        for copy in copies[4:]:
            copy.wait()
        pair = 2 * width // HEADS
        limit = lengths[table_index]
        cached = lax.broadcasted_iota(jnp.int32, keys.shape[1:], 0) < limit
        first = lax.broadcasted_iota(jnp.int32, (tile, pair), 1) < pair // 2
        scale = 0.5 * (width // HEADS) ** -0.5
        for layer in range(w_proj.shape[0]):
            normed = jnp.concatenate(
                [
                    block.astype(jnp.bfloat16)
                    for block in normalized(in_blocks(states.astype(jnp.float32)))
                ],
                axis=1,
            )
            queries = half_silu(dot(normed, w_proj[layer, :, width:]) * 0.5) * scale
            queries = queries.astype(jnp.bfloat16)
            kept = jnp.where(cached, keys[layer], jnp.zeros((), jnp.bfloat16))

            def score(block):
                query = queries[:, block * pair : (block + 1) * pair]
                none = jnp.zeros((), jnp.bfloat16)
                both = jnp.concatenate(
                    [jnp.where(first, query, none), jnp.where(first, none, query)], axis=0
                )
                return dot_rows(both, kept[:, block * pair : (block + 1) * pair])

            attended = []
            scores = score(0)
            for block in range(HEADS // 2):
                following = score(block + 1) if block + 1 < HEADS // 2 else None
                weighted = half_silu(scores).astype(jnp.bfloat16)
                both = dot(weighted, values[layer, :, block * pair : (block + 1) * pair])
                attended.append(jnp.where(first, both[:tile], both[tile:]))
                scores = following
            gate = half_silu(dot(normed, w_proj[layer, :, :width]) * 0.5)
            mixed = [
                (block * open_).astype(jnp.bfloat16)
                for block, open_ in zip(normalized(attended), in_blocks(gate))
            ]
            mixed = jnp.concatenate(mixed, axis=1)
            states = (states.astype(jnp.float32) + dot(mixed, w_back[layer])).astype(jnp.bfloat16)
        keep(states)

    if done:

        @pl.when(low >= filled)
        def _():
            fill_before()
            fill_slots(True)

        fill_slots(False)
        for sender in range(groups):
            put(sender).wait()


def rank(counts, lengths, pieces, before, history, weights, low, capacity):
    groups, part, _ = pieces.shape
    width = weights[0].shape[0]
    tile = part * groups * LANES // width
    total = groups * capacity
    done = len(before)
    layers, piece_rows, _ = history[0].shape
    shards = len(history) // 2
    scratch = [pltpu.VMEM(pieces.shape, pieces.dtype)]
    scratch += [pltpu.VMEM((layers, shards * piece_rows, width), jnp.bfloat16)] * 2
    scratch += [pltpu.VMEM(weight.shape, weight.dtype) for weight in weights]
    scratch += [pltpu.SemaphoreType.DMA((len(weights) + 3 + len(history) + done,))]
    if done:
        scratch = [pltpu.VMEM((width // LANES, total + capacity, LANES), jnp.float32)] + scratch
        scratch += [pltpu.VMEM(piece.shape, piece.dtype) for piece in before]
        scratch += [pltpu.VMEM((total, width), jnp.bfloat16), pltpu.SemaphoreType.DMA((groups,))]
    return pl.pallas_call(
        functools.partial(rank_kernel, low, capacity, done, shards),
        out_shape=jax.ShapeDtypeStruct((total if done else tile, width), jnp.bfloat16),
        in_specs=[SMEM, SMEM] + [ANY] * (1 + done + len(history) + len(weights)),
        out_specs=ANY if done else VMEM,
        scratch_shapes=scratch,
        compiler_params=pltpu.CompilerParams(vmem_limit_bytes=64 * MIB - MIB // 4),
        cost_estimate=pl.CostEstimate(
            flops=20_000_000_000, bytes_accessed=20_000_000, transcendentals=0
        ),
        name="rank",
    )(counts, lengths, pieces, *before, *history, *weights)


def local(item_ids, item_table, group_counts, lengths, history, w_in, w_out, w_proj, w_back):
    groups = lax.axis_size("table")
    row_count = item_ids.shape[0] // groups
    capacity = 3 * row_count // (2 * groups)
    total = groups * capacity
    cuts = (0, total // 2, total)
    table_t = item_table.T
    found = lookup(item_ids, group_counts, table_t, cuts)
    pieces = [
        lax.all_to_all(chunk, "table", split_axis=0, concat_axis=0, tiled=True) for chunk in found
    ]
    history = gather_history(history)
    weights = (w_in, w_out, w_proj, w_back)
    states = []
    for low, chunk in zip(cuts, pieces):
        before = states if low == cuts[-2] else []
        states = states + [
            rank(group_counts, lengths, chunk, before, history, weights, low, capacity)
        ]
    return states[-1]


def solution(mesh):
    placed = (
        P("seq"),
        P("seq", "table"),
        P(),
        P(),
        P("table", None, None, "seq", None),
        P(),
        P(),
        P(),
        P(),
    )
    return jax.shard_map(
        local, mesh=mesh, in_specs=placed, out_specs=P(("table", "seq"), None), check_vma=False
    )
```

```python
import functools

import jax
import jax.numpy as jnp
from jax import lax
from jax.experimental import pallas as pl
from jax.experimental.pallas import tpu as pltpu
from jax.sharding import PartitionSpec as P

HEADS = 8
LANES = 128
UNROLL = 256
MIB = 1 << 20
ANY = pl.BlockSpec(memory_space=pl.ANY)
SMEM = pl.BlockSpec(memory_space=pltpu.SMEM)
VMEM = pl.BlockSpec(memory_space=pltpu.VMEM)


def lookup_kernel(cuts, ids, counts, table_t, *refs):
    chunks = len(cuts) - 1
    outs, packed, put_sems, refs = refs[:chunks], refs[-chunks - 1 : -1], refs[-1], refs[chunks : -chunks - 1]
    table, rows_major, found, picked, id_vector, local_ids, held, sems = refs
    columns, vocab = table_t.shape
    groups = counts.shape[0]
    id_count = ids.shape[0]
    row_count = id_count // groups
    packing = LANES // columns
    capacity = cuts[-1] // groups
    shard = lax.axis_index("seq")
    get_ids = pltpu.make_async_copy(ids, id_vector, sems.at[0])
    get_ids.start()
    get_counts = pltpu.make_async_copy(counts, held, sems.at[1])
    get_counts.start()
    parts = 8
    block = vocab // parts
    get_table = [
        pltpu.make_async_copy(
            table_t.at[:, pl.ds(part * block, block)],
            table.at[:, pl.ds(part * block, block)],
            sems.at[3 + part],
        )
        for part in range(parts)
    ]
    for copy in get_table:
        copy.start()
    get_ids.wait()
    id_vector[...] = id_vector[...] - shard * vocab
    put_ids = pltpu.make_async_copy(id_vector, local_ids, sems.at[2])
    put_ids.start()
    for part in range(parts):
        get_table[part].wait()
        piece = table[:, part * block : (part + 1) * block]
        piece = jnp.concatenate([piece] * packing, axis=0)
        rows_major[pl.ds(part * block, block), :] = piece.T.astype(jnp.float32)
    get_counts.wait()
    put_ids.wait()

    def gather(step, carry):
        at = pl.multiple_of(step * UNROLL, UNROLL)
        rows = [rows_major[pl.ds(local_ids[at + k], 1), :] for k in range(UNROLL)]
        for k in range(UNROLL):
            found[pl.ds(at + k, 1), :] = rows[k]
        return carry

    lax.fori_loop(0, id_count // UNROLL, gather, 0)

    def sender(sender_id, starts):
        source = sender_id * row_count
        new_starts = []
        for group in range(groups):
            amount = held[sender_id, shard, group]
            picked[group, pl.ds(starts[group], capacity), :] = found[pl.ds(source, capacity), :]
            source = source + amount
            new_starts.append(starts[group] + amount)
        return tuple(new_starts)

    lax.fori_loop(0, groups, sender, (jnp.int32(0),) * groups)

    puts = []
    for chunk, (low, out) in enumerate(zip(cuts, outs)):
        part = out.shape[1]
        lane = lax.broadcasted_iota(jnp.int32, (part, LANES), 1) // columns
        for group in range(groups):
            value = picked[group, pl.ds(low, part), :]
            for piece in range(1, packing):
                more = picked[group, pl.ds(low + piece * part, part), :]
                value = jnp.where(lane == piece, more, value)
            packed[chunk][group] = value.astype(jnp.bfloat16)
            puts.append(
                pltpu.make_async_copy(
                    packed[chunk].at[group], out.at[group], put_sems.at[len(puts)]
                )
            )
            puts[-1].start()
    for copy in puts:
        copy.wait()


def lookup(ids, counts, table_t, cuts):
    columns, vocab = table_t.shape
    packing = LANES // columns
    groups = counts.shape[0]
    total = cuts[-1]
    return pl.pallas_call(
        functools.partial(lookup_kernel, cuts),
        out_shape=tuple(
            jax.ShapeDtypeStruct((groups, (high - low) // packing, LANES), jnp.bfloat16)
            for low, high in zip(cuts, cuts[1:])
        ),
        in_specs=[ANY, ANY, ANY],
        out_specs=(ANY,) * (len(cuts) - 1),
        scratch_shapes=[
            pltpu.VMEM((columns, vocab), jnp.bfloat16),
            pltpu.VMEM((vocab, LANES), jnp.float32),
            pltpu.VMEM((ids.shape[0] + total // groups, LANES), jnp.float32),
            pltpu.VMEM((groups, total + total // groups, LANES), jnp.float32),
            pltpu.VMEM(ids.shape, jnp.int32),
            pltpu.SMEM(ids.shape, jnp.int32),
            pltpu.SMEM(counts.shape, jnp.int32),
            pltpu.SemaphoreType.DMA((11,)),
        ]
        + [
            pltpu.VMEM((groups, (high - low) // packing, LANES), jnp.bfloat16)
            for low, high in zip(cuts, cuts[1:])
        ]
        + [pltpu.SemaphoreType.DMA((groups * (len(cuts) - 1),))],
        compiler_params=pltpu.CompilerParams(vmem_limit_bytes=64 * MIB - MIB // 4),
        name="lookup",
    )(ids, counts, table_t)


def gather_history(history):
    shards = lax.axis_size("seq")
    bits = [1 << k for k in range(shards.bit_length() - 1)]
    pieces = []
    for kind in range(2):
        held = {0: history[0, :, kind]}
        for bit in bits if kind == 0 else bits[::-1]:
            route = [(i, i ^ bit) for i in range(shards)]
            held.update({k ^ bit: lax.ppermute(v, "seq", route) for k, v in list(held.items())})
        pieces += [held[index] for index in range(shards)]
    return pieces


def half_silu(half):
    return half + half * jnp.tanh(half)


def dot(left, right):
    return jnp.dot(left, right, preferred_element_type=jnp.float32)


def dot_rows(left, right):
    return lax.dot_general(
        left, right, (((1,), (1,)), ((), ())), preferred_element_type=jnp.float32
    )


def row_mean(blocks):
    partial = sum(blocks[1:], blocks[0])
    high = partial.astype(jnp.bfloat16)
    low = (partial - high.astype(jnp.float32)).astype(jnp.bfloat16)
    ones = jnp.full((2 * LANES, LANES), 1.0 / (LANES * len(blocks)), jnp.bfloat16)
    return dot(jnp.concatenate([high, low], axis=1), ones)


def normalized(blocks):
    mean = row_mean(blocks)
    centred = [block - mean for block in blocks]
    factor = lax.rsqrt(row_mean([block * block for block in centred]) + 1e-06)
    return [block * factor for block in centred]


def in_blocks(values):
    return [values[:, at : at + LANES] for at in range(0, values.shape[1], LANES)]


def rank_kernel(low, capacity, done, shards, counts_in_hbm, lengths_in_hbm, pieces, *refs):
    before, refs = refs[:done], refs[done:]
    history, refs = refs[: 2 * shards], refs[2 * shards :]
    weights, out, refs = refs[:4], refs[4], refs[5:]
    ranked, refs = (refs[0], refs[1:]) if done else (None, refs)
    counts, lengths, refs = refs[0], refs[1], refs[2:]
    got, keys, values, w_in, w_out, w_proj, w_back, sems, refs = *refs[:8], refs[8:]
    pieces_in_hbm, pieces = pieces, got
    groups, part, _ = pieces.shape
    width = w_in.shape[0]
    packing = groups * LANES // width
    columns = LANES // packing
    tile = part * packing
    table_index = lax.axis_index("table")
    shard = lax.axis_index("seq")
    last_sem = sems.shape[0] - 1
    get_numbers = [
        pltpu.make_async_copy(counts_in_hbm, counts, sems.at[last_sem]),
        pltpu.make_async_copy(lengths_in_hbm, lengths, sems.at[last_sem - 1]),
    ]
    for copy in get_numbers:
        copy.start()
    get_pieces = pltpu.make_async_copy(pieces_in_hbm, pieces, sems.at[last_sem - 2])
    get_before = []
    for k, piece in enumerate(before):
        get_before.append(pltpu.make_async_copy(piece, refs[k], sems.at[last_sem - 3 - k]))
        get_before[-1].start()

    chunk = width
    head, tail = pl.ds(0, chunk), pl.ds(chunk, w_in.shape[1] - chunk)
    views = [
        (weights[0].at[:, head], w_in.at[:, head]),
        (weights[1].at[head], w_out.at[head]),
        (weights[0].at[:, tail], w_in.at[:, tail]),
        (weights[1].at[tail], w_out.at[tail]),
        (weights[2], w_proj),
        (weights[3], w_back),
    ]
    piece_rows = keys.shape[1] // shards
    for k in range(2 * shards):
        place = pl.multiple_of((shard ^ (k % shards)) * piece_rows, piece_rows)
        target = (keys, values)[k // shards]
        views.append((history[k], target.at[:, pl.ds(place, piece_rows), :]))
    copies = [
        pltpu.make_async_copy(source, target, sems.at[k])
        for k, (source, target) in enumerate(views)
    ]
    copies[0].start()
    get_pieces.start()
    for copy in copies[1:4]:
        copy.start()
    for copy in get_numbers:
        copy.wait()
    filled = lax.fori_loop(
        0, groups, lambda t, n: n + counts[t, shard, table_index], jnp.int32(0)
    )

    def keep(states):
        if done:
            for block in range(width // LANES):
                ranked[block, pl.ds(low, tile), :] = states[
                    :, block * LANES : (block + 1) * LANES
                ].astype(jnp.float32)
        else:
            out[...] = states

    if done:
        slots, put_sems = refs[done], refs[done + 1]
        slot_row = lax.broadcasted_iota(jnp.int32, (capacity, LANES), 0)

    def put(sender):
        place = pl.ds(pl.multiple_of(sender * capacity, capacity), capacity)
        return pltpu.make_async_copy(slots.at[place], out.at[place], put_sems.at[sender])

    def fill_before():
        at = 0
        for copy, piece in zip(get_before, refs):
            copy.wait()
            for block in range(width // LANES):
                ranked[block, pl.ds(at, piece.shape[0]), :] = piece[
                    :, pl.ds(block * LANES, LANES)
                ].astype(jnp.float32)
            at += piece.shape[0]

    def fill_slots(early):
        def slot_block(sender, start):
            amount = counts[sender, shard, table_index]

            @pl.when((start + amount <= low) == early)
            def _():
                for block in range(width // LANES):
                    value = ranked[block, pl.ds(start, capacity), :]
                    slots[
                        pl.ds(pl.multiple_of(sender * capacity, capacity), capacity),
                        block * LANES : (block + 1) * LANES,
                    ] = jnp.where(slot_row < amount, value, 0.0).astype(jnp.bfloat16)
                put(sender).start()

            return start + amount

        lax.fori_loop(0, groups, slot_block, jnp.int32(0))

    @pl.when(low < filled)
    def _():
        if done:
            fill_before()
            fill_slots(True)
        get_pieces.wait()
        lane = lax.broadcasted_iota(jnp.int32, (part, LANES), 1) // columns
        row = lax.broadcasted_iota(jnp.int32, (part, LANES), 0)
        rows = []
        for piece in range(packing):
            wanted = row + (low + piece * part) < filled
            blocks = []
            for block in range(width // LANES):
                value = None
                for spot in range(packing):
                    source = pieces[block * packing + spot].astype(jnp.float32)
                    turn = (spot - piece) % packing * columns
                    if turn:
                        source = pltpu.roll(source, turn, 1)
                    value = source if value is None else jnp.where(lane == spot, source, value)
                blocks.append(jnp.where(wanted, value, 0.0))
            rows.append(jnp.concatenate(blocks, axis=1))
        embedded = jnp.concatenate(rows, axis=0)
        embedded16 = embedded.astype(jnp.bfloat16)
        total = embedded
        for copy in copies[:2]:
            copy.wait()
        for copy in copies[4:]:
            copy.start()
        for at in range(0, w_in.shape[1], chunk):
            if at == chunk:
                for copy in copies[2:4]:
                    copy.wait()
            half = dot(embedded16, w_in[:, at : at + chunk]) * 0.5
            hidden = half_silu(half).astype(jnp.bfloat16)
            total = total + dot(hidden, w_out[at : at + chunk, :])
        states = total.astype(jnp.bfloat16)
        for copy in copies[4:]:
            copy.wait()
        pair = 2 * width // HEADS
        limit = lengths[table_index]
        cached = lax.broadcasted_iota(jnp.int32, keys.shape[1:], 0) < limit
        first = lax.broadcasted_iota(jnp.int32, (tile, pair), 1) < pair // 2
        scale = 0.5 * (width // HEADS) ** -0.5
        for layer in range(w_proj.shape[0]):
            normed = jnp.concatenate(
                [
                    block.astype(jnp.bfloat16)
                    for block in normalized(in_blocks(states.astype(jnp.float32)))
                ],
                axis=1,
            )
            queries = half_silu(dot(normed, w_proj[layer, :, width:]) * 0.5) * scale
            queries = queries.astype(jnp.bfloat16)
            kept = jnp.where(cached, keys[layer], jnp.zeros((), jnp.bfloat16))

            def score(block):
                query = queries[:, block * pair : (block + 1) * pair]
                none = jnp.zeros((), jnp.bfloat16)
                both = jnp.concatenate(
                    [jnp.where(first, query, none), jnp.where(first, none, query)], axis=0
                )
                return dot_rows(both, kept[:, block * pair : (block + 1) * pair])

            attended = []
            scores = score(0)
            for block in range(HEADS // 2):
                following = score(block + 1) if block + 1 < HEADS // 2 else None
                weighted = half_silu(scores).astype(jnp.bfloat16)
                both = dot(weighted, values[layer, :, block * pair : (block + 1) * pair])
                attended.append(jnp.where(first, both[:tile], both[tile:]))
                scores = following
            gate = half_silu(dot(normed, w_proj[layer, :, :width]) * 0.5)
            mixed = [
                (block * open_).astype(jnp.bfloat16)
                for block, open_ in zip(normalized(attended), in_blocks(gate))
            ]
            mixed = jnp.concatenate(mixed, axis=1)
            states = (states.astype(jnp.float32) + dot(mixed, w_back[layer])).astype(jnp.bfloat16)
        keep(states)

    @pl.when(low >= filled)
    def _():
        for copy in copies[:4]:
            copy.wait()
        get_pieces.wait()
        if done:
            fill_before()
            fill_slots(True)

    if done:
        fill_slots(False)
        for sender in range(groups):
            put(sender).wait()


def rank(counts, lengths, pieces, before, history, weights, low, capacity):
    groups, part, _ = pieces.shape
    width = weights[0].shape[0]
    tile = part * groups * LANES // width
    total = groups * capacity
    done = len(before)
    layers, piece_rows, _ = history[0].shape
    shards = len(history) // 2
    numbers = [pltpu.SMEM(counts.shape, jnp.int32), pltpu.SMEM(lengths.shape, jnp.int32)]
    scratch = numbers + [pltpu.VMEM(pieces.shape, pieces.dtype)]
    scratch += [pltpu.VMEM((layers, shards * piece_rows, width), jnp.bfloat16)] * 2
    scratch += [pltpu.VMEM(weight.shape, weight.dtype) for weight in weights]
    scratch += [pltpu.SemaphoreType.DMA((len(weights) + 5 + len(history) + done,))]
    if done:
        scratch = [pltpu.VMEM((width // LANES, total + capacity, LANES), jnp.float32)] + scratch
        scratch += [pltpu.VMEM(piece.shape, piece.dtype) for piece in before]
        scratch += [pltpu.VMEM((total, width), jnp.bfloat16), pltpu.SemaphoreType.DMA((groups,))]
    return pl.pallas_call(
        functools.partial(rank_kernel, low, capacity, done, shards),
        out_shape=jax.ShapeDtypeStruct((total if done else tile, width), jnp.bfloat16),
        in_specs=[ANY] * (3 + done + len(history) + len(weights)),
        out_specs=ANY if done else VMEM,
        scratch_shapes=scratch,
        compiler_params=pltpu.CompilerParams(vmem_limit_bytes=64 * MIB - MIB // 4),
        cost_estimate=pl.CostEstimate(
            flops=20_000_000_000, bytes_accessed=20_000_000, transcendentals=0
        ),
        name="rank",
    )(counts, lengths, pieces, *before, *history, *weights)


def local(item_ids, item_table, group_counts, lengths, history, w_in, w_out, w_proj, w_back):
    groups = lax.axis_size("table")
    row_count = item_ids.shape[0] // groups
    capacity = 3 * row_count // (2 * groups)
    total = groups * capacity
    packing = LANES // item_table.shape[1]
    cuts = (0, total * 25 // 48 // (16 * packing) * (16 * packing), total)
    table_t = item_table.T
    found = lookup(item_ids, group_counts, table_t, cuts)
    pieces = [
        lax.all_to_all(chunk, "table", split_axis=0, concat_axis=0, tiled=True) for chunk in found
    ]
    history = gather_history(history)
    weights = (w_in, w_out, w_proj, w_back)
    states = []
    for low, chunk in zip(cuts, pieces):
        before = states if low == cuts[-2] else []
        states = states + [
            rank(group_counts, lengths, chunk, before, history, weights, low, capacity)
        ]
    return states[-1]


def solution(mesh):
    placed = (
        P("seq"),
        P("seq", "table"),
        P(),
        P(),
        P("table", None, None, "seq", None),
        P(),
        P(),
        P(),
        P(),
    )
    return jax.shard_map(
        local, mesh=mesh, in_specs=placed, out_specs=P(("table", "seq"), None), check_vma=False
    )
```

```python
import functools

import jax
import jax.numpy as jnp
from jax import lax
from jax.experimental import pallas as pl
from jax.experimental.pallas import tpu as pltpu
from jax.sharding import PartitionSpec as P

HEADS = 8
LANES = 128
UNROLL = 256
MIB = 1 << 20
ANY = pl.BlockSpec(memory_space=pl.ANY)
SMEM = pl.BlockSpec(memory_space=pltpu.SMEM)
VMEM = pl.BlockSpec(memory_space=pltpu.VMEM)


def lookup_kernel(cuts, ids, counts, table_t, *refs):
    chunks = len(cuts) - 1
    outs, packed, put_sems, refs = refs[:chunks], refs[-chunks - 1 : -1], refs[-1], refs[chunks : -chunks - 1]
    table, rows_major, found, picked, id_vector, local_ids, held, sems = refs
    columns, vocab = table_t.shape
    groups = counts.shape[0]
    id_count = ids.shape[0]
    row_count = id_count // groups
    packing = LANES // columns
    capacity = cuts[-1] // groups
    shard = lax.axis_index("seq")
    get_ids = pltpu.make_async_copy(ids, id_vector, sems.at[0])
    get_ids.start()
    get_counts = pltpu.make_async_copy(counts, held, sems.at[1])
    get_counts.start()
    parts = 8
    block = vocab // parts
    get_table = [
        pltpu.make_async_copy(
            table_t.at[:, pl.ds(part * block, block)],
            table.at[:, pl.ds(part * block, block)],
            sems.at[3 + part],
        )
        for part in range(parts)
    ]
    for copy in get_table:
        copy.start()
    get_ids.wait()
    id_vector[...] = id_vector[...] - shard * vocab
    put_ids = pltpu.make_async_copy(id_vector, local_ids, sems.at[2])
    put_ids.start()
    for part in range(parts):
        get_table[part].wait()
        piece = table[:, part * block : (part + 1) * block]
        piece = jnp.concatenate([piece] * packing, axis=0)
        rows_major[pl.ds(part * block, block), :] = piece.T.astype(jnp.float32)
    get_counts.wait()
    put_ids.wait()

    def gather(step, carry):
        at = pl.multiple_of(step * UNROLL, UNROLL)
        rows = [rows_major[pl.ds(local_ids[at + k], 1), :] for k in range(UNROLL)]
        for k in range(UNROLL):
            found[pl.ds(at + k, 1), :] = rows[k]
        return carry

    lax.fori_loop(0, id_count // UNROLL, gather, 0)

    def sender(sender_id, starts):
        source = sender_id * row_count
        new_starts = []
        for group in range(groups):
            amount = held[sender_id, shard, group]
            picked[group, pl.ds(starts[group], capacity), :] = found[pl.ds(source, capacity), :]
            source = source + amount
            new_starts.append(starts[group] + amount)
        return tuple(new_starts)

    lax.fori_loop(0, groups, sender, (jnp.int32(0),) * groups)

    puts = []
    for chunk, (low, out) in enumerate(zip(cuts, outs)):
        part = out.shape[1]
        lane = lax.broadcasted_iota(jnp.int32, (part, LANES), 1) // columns
        for group in range(groups):
            value = picked[group, pl.ds(low, part), :]
            for piece in range(1, packing):
                more = picked[group, pl.ds(low + piece * part, part), :]
                value = jnp.where(lane == piece, more, value)
            packed[chunk][group] = value.astype(jnp.bfloat16)
            puts.append(
                pltpu.make_async_copy(
                    packed[chunk].at[group], out.at[group], put_sems.at[len(puts)]
                )
            )
            puts[-1].start()
    for copy in puts:
        copy.wait()


def lookup(ids, counts, table_t, cuts):
    columns, vocab = table_t.shape
    packing = LANES // columns
    groups = counts.shape[0]
    total = cuts[-1]
    return pl.pallas_call(
        functools.partial(lookup_kernel, cuts),
        out_shape=tuple(
            jax.ShapeDtypeStruct((groups, (high - low) // packing, LANES), jnp.bfloat16)
            for low, high in zip(cuts, cuts[1:])
        ),
        in_specs=[ANY, ANY, ANY],
        out_specs=(ANY,) * (len(cuts) - 1),
        scratch_shapes=[
            pltpu.VMEM((columns, vocab), jnp.bfloat16),
            pltpu.VMEM((vocab, LANES), jnp.float32),
            pltpu.VMEM((ids.shape[0] + total // groups, LANES), jnp.float32),
            pltpu.VMEM((groups, total + total // groups, LANES), jnp.float32),
            pltpu.VMEM(ids.shape, jnp.int32),
            pltpu.SMEM(ids.shape, jnp.int32),
            pltpu.SMEM(counts.shape, jnp.int32),
            pltpu.SemaphoreType.DMA((11,)),
        ]
        + [
            pltpu.VMEM((groups, (high - low) // packing, LANES), jnp.bfloat16)
            for low, high in zip(cuts, cuts[1:])
        ]
        + [pltpu.SemaphoreType.DMA((groups * (len(cuts) - 1),))],
        compiler_params=pltpu.CompilerParams(vmem_limit_bytes=64 * MIB - MIB // 4),
        name="lookup",
    )(ids, counts, table_t)


def gather_history(history):
    shards = lax.axis_size("seq")
    bits = [1 << k for k in range(shards.bit_length() - 1)]
    pieces = []
    for kind in range(2):
        held = {0: history[0, :, kind]}
        for bit in bits if kind == 0 else bits[::-1]:
            route = [(i, i ^ bit) for i in range(shards)]
            held.update({k ^ bit: lax.ppermute(v, "seq", route) for k, v in list(held.items())})
        pieces += [held[index] for index in range(shards)]
    return pieces


def half_silu(half):
    return half + half * jnp.tanh(half)


def dot(left, right):
    return jnp.dot(left, right, preferred_element_type=jnp.float32)


def dot_rows(left, right):
    return lax.dot_general(
        left, right, (((1,), (1,)), ((), ())), preferred_element_type=jnp.float32
    )


def row_mean(blocks):
    partial = sum(blocks[1:], blocks[0])
    high = partial.astype(jnp.bfloat16)
    low = (partial - high.astype(jnp.float32)).astype(jnp.bfloat16)
    ones = jnp.full((2 * LANES, LANES), 1.0 / (LANES * len(blocks)), jnp.bfloat16)
    return dot(jnp.concatenate([high, low], axis=1), ones)


def normalized(blocks):
    mean = row_mean(blocks)
    centred = [block - mean for block in blocks]
    factor = lax.rsqrt(row_mean([block * block for block in centred]) + 1e-06)
    return [block * factor for block in centred]


def in_blocks(values):
    return [values[:, at : at + LANES] for at in range(0, values.shape[1], LANES)]


def rank_kernel(low, capacity, done, shards, counts_in_hbm, lengths_in_hbm, pieces, *refs):
    before, refs = refs[:done], refs[done:]
    history, refs = refs[: 2 * shards], refs[2 * shards :]
    weights, out, refs = refs[:4], refs[4], refs[5:]
    ranked, refs = (refs[0], refs[1:]) if done else (None, refs)
    counts, lengths, refs = refs[0], refs[1], refs[2:]
    got, keys, values, w_in, w_out, w_proj, w_back, sems, refs = *refs[:8], refs[8:]
    pieces_in_hbm, pieces = pieces, got
    groups, part, _ = pieces.shape
    width = w_in.shape[0]
    packing = groups * LANES // width
    columns = LANES // packing
    tile = part * packing
    table_index = lax.axis_index("table")
    shard = lax.axis_index("seq")
    last_sem = sems.shape[0] - 1
    get_numbers = [
        pltpu.make_async_copy(counts_in_hbm, counts, sems.at[last_sem]),
        pltpu.make_async_copy(lengths_in_hbm, lengths, sems.at[last_sem - 1]),
    ]
    for copy in get_numbers:
        copy.start()
    get_pieces = pltpu.make_async_copy(pieces_in_hbm, pieces, sems.at[last_sem - 2])
    get_before = []
    for k, piece in enumerate(before):
        get_before.append(pltpu.make_async_copy(piece, refs[k], sems.at[last_sem - 3 - k]))
        get_before[-1].start()

    chunk = width
    head, tail = pl.ds(0, chunk), pl.ds(chunk, w_in.shape[1] - chunk)
    views = [
        (weights[0].at[:, head], w_in.at[:, head]),
        (weights[1].at[head], w_out.at[head]),
        (weights[0].at[:, tail], w_in.at[:, tail]),
        (weights[1].at[tail], w_out.at[tail]),
        (weights[2], w_proj),
        (weights[3], w_back),
    ]
    piece_rows = keys.shape[1] // shards
    for k in range(2 * shards):
        place = pl.multiple_of((shard ^ (k % shards)) * piece_rows, piece_rows)
        target = (keys, values)[k // shards]
        views.append((history[k], target.at[:, pl.ds(place, piece_rows), :]))
    copies = [
        pltpu.make_async_copy(source, target, sems.at[k])
        for k, (source, target) in enumerate(views)
    ]
    copies[0].start()
    get_pieces.start()
    for copy in copies[1:4]:
        copy.start()
    for copy in get_numbers:
        copy.wait()
    filled = lax.fori_loop(
        0, groups, lambda t, n: n + counts[t, shard, table_index], jnp.int32(0)
    )

    def keep(states):
        for block in range(width // LANES):
            ranked[block, pl.ds(low, tile), :] = states[
                :, block * LANES : (block + 1) * LANES
            ].astype(jnp.float32)

    if done:
        slots, put_sems = refs[done], refs[done + 1]
        slot_row = lax.broadcasted_iota(jnp.int32, (capacity, LANES), 0)

    def put(sender):
        place = pl.ds(pl.multiple_of(sender * capacity, capacity), capacity)
        return pltpu.make_async_copy(slots.at[place], out.at[place], put_sems.at[sender])

    def fill_before():
        at = 0
        for copy, piece in zip(get_before, refs):
            copy.wait()
            for block in range(width // LANES):
                ranked[block, pl.ds(at, piece.shape[0]), :] = piece[
                    :, pl.ds(block * LANES, LANES)
                ].astype(jnp.float32)
            at += piece.shape[0]

    def fill_slots(early):
        def slot_block(sender, start):
            amount = counts[sender, shard, table_index]

            @pl.when((start + amount <= low) == early)
            def _():
                for block in range(width // LANES):
                    value = ranked[block, pl.ds(start, capacity), :]
                    slots[
                        pl.ds(pl.multiple_of(sender * capacity, capacity), capacity),
                        block * LANES : (block + 1) * LANES,
                    ] = jnp.where(slot_row < amount, value, 0.0).astype(jnp.bfloat16)
                put(sender).start()

            return start + amount

        lax.fori_loop(0, groups, slot_block, jnp.int32(0))

    @pl.when(low < filled)
    def _():
        if done:
            fill_before()
            fill_slots(True)
        get_pieces.wait()
        lane = lax.broadcasted_iota(jnp.int32, (part, LANES), 1) // columns
        row = lax.broadcasted_iota(jnp.int32, (part, LANES), 0)
        rows = []
        for piece in range(packing):
            wanted = row + (low + piece * part) < filled
            blocks = []
            for block in range(width // LANES):
                value = None
                for spot in range(packing):
                    source = pieces[block * packing + spot].astype(jnp.float32)
                    turn = (spot - piece) % packing * columns
                    if turn:
                        source = pltpu.roll(source, turn, 1)
                    value = source if value is None else jnp.where(lane == spot, source, value)
                blocks.append(jnp.where(wanted, value, 0.0))
            rows.append(jnp.concatenate(blocks, axis=1))
        embedded = jnp.concatenate(rows, axis=0)
        embedded16 = embedded.astype(jnp.bfloat16)
        total = embedded
        for copy in copies[:2]:
            copy.wait()
        for copy in copies[4:]:
            copy.start()
        for at in range(0, w_in.shape[1], chunk):
            if at == chunk:
                for copy in copies[2:4]:
                    copy.wait()
            half = dot(embedded16, w_in[:, at : at + chunk]) * 0.5
            hidden = half_silu(half).astype(jnp.bfloat16)
            total = total + dot(hidden, w_out[at : at + chunk, :])
        states = total.astype(jnp.bfloat16)
        for copy in copies[4:]:
            copy.wait()
        pair = 2 * width // HEADS
        limit = lengths[table_index]
        cached = lax.broadcasted_iota(jnp.int32, keys.shape[1:], 0) < limit
        first = lax.broadcasted_iota(jnp.int32, (tile, pair), 1) < pair // 2
        scale = 0.5 * (width // HEADS) ** -0.5
        for layer in range(w_proj.shape[0]):
            normed = jnp.concatenate(
                [
                    block.astype(jnp.bfloat16)
                    for block in normalized(in_blocks(states.astype(jnp.float32)))
                ],
                axis=1,
            )
            queries = half_silu(dot(normed, w_proj[layer, :, width:]) * 0.5) * scale
            queries = queries.astype(jnp.bfloat16)
            kept = jnp.where(cached, keys[layer], jnp.zeros((), jnp.bfloat16))

            def score(block):
                query = queries[:, block * pair : (block + 1) * pair]
                none = jnp.zeros((), jnp.bfloat16)
                both = jnp.concatenate(
                    [jnp.where(first, query, none), jnp.where(first, none, query)], axis=0
                )
                return dot_rows(both, kept[:, block * pair : (block + 1) * pair])

            attended = []
            scores = score(0)
            for block in range(HEADS // 2):
                following = score(block + 1) if block + 1 < HEADS // 2 else None
                weighted = half_silu(scores).astype(jnp.bfloat16)
                both = dot(weighted, values[layer, :, block * pair : (block + 1) * pair])
                attended.append(jnp.where(first, both[:tile], both[tile:]))
                scores = following
            gate = half_silu(dot(normed, w_proj[layer, :, :width]) * 0.5)
            mixed = [
                (block * open_).astype(jnp.bfloat16)
                for block, open_ in zip(normalized(attended), in_blocks(gate))
            ]
            mixed = jnp.concatenate(mixed, axis=1)
            if layer + 1 == w_proj.shape[0] and not done:
                continue
            states = (states.astype(jnp.float32) + dot(mixed, w_back[layer])).astype(jnp.bfloat16)
        if done:
            keep(states)
        else:
            staged, put_sems = refs
            puts = []
            middle = tile // 32 * 16
            for k, (at, end) in enumerate(((0, middle), (middle, tile))):
                more = dot(mixed[at:end], w_back[w_proj.shape[0] - 1])
                rows = pl.ds(at, end - at)
                staged[rows, :] = (states[at:end].astype(jnp.float32) + more).astype(jnp.bfloat16)
                puts.append(
                    pltpu.make_async_copy(staged.at[rows], out.at[rows], put_sems.at[k])
                )
                puts[-1].start()
            for copy in puts:
                copy.wait()

    @pl.when(low >= filled)
    def _():
        for copy in copies[:4]:
            copy.wait()
        get_pieces.wait()
        if done:
            fill_before()
            fill_slots(True)

    if done:
        fill_slots(False)
        for sender in range(groups):
            put(sender).wait()


def rank(counts, lengths, pieces, before, history, weights, low, capacity):
    groups, part, _ = pieces.shape
    width = weights[0].shape[0]
    tile = part * groups * LANES // width
    total = groups * capacity
    done = len(before)
    layers, piece_rows, _ = history[0].shape
    shards = len(history) // 2
    numbers = [pltpu.SMEM(counts.shape, jnp.int32), pltpu.SMEM(lengths.shape, jnp.int32)]
    scratch = numbers + [pltpu.VMEM(pieces.shape, pieces.dtype)]
    scratch += [pltpu.VMEM((layers, shards * piece_rows, width), jnp.bfloat16)] * 2
    scratch += [pltpu.VMEM(weight.shape, weight.dtype) for weight in weights]
    scratch += [pltpu.SemaphoreType.DMA((len(weights) + 5 + len(history) + done,))]
    if done:
        scratch = [pltpu.VMEM((width // LANES, total + capacity, LANES), jnp.float32)] + scratch
        scratch += [pltpu.VMEM(piece.shape, piece.dtype) for piece in before]
        scratch += [pltpu.VMEM((total, width), jnp.bfloat16), pltpu.SemaphoreType.DMA((groups,))]
    else:
        scratch += [pltpu.VMEM((tile, width), jnp.bfloat16), pltpu.SemaphoreType.DMA((2,))]
    return pl.pallas_call(
        functools.partial(rank_kernel, low, capacity, done, shards),
        out_shape=jax.ShapeDtypeStruct((total if done else tile, width), jnp.bfloat16),
        in_specs=[ANY] * (3 + done + len(history) + len(weights)),
        out_specs=ANY,
        scratch_shapes=scratch,
        compiler_params=pltpu.CompilerParams(vmem_limit_bytes=64 * MIB - MIB // 4),
        cost_estimate=pl.CostEstimate(
            flops=20_000_000_000, bytes_accessed=20_000_000, transcendentals=0
        ),
        name="rank",
    )(counts, lengths, pieces, *before, *history, *weights)


def local(item_ids, item_table, group_counts, lengths, history, w_in, w_out, w_proj, w_back):
    groups = lax.axis_size("table")
    row_count = item_ids.shape[0] // groups
    capacity = 3 * row_count // (2 * groups)
    total = groups * capacity
    packing = LANES // item_table.shape[1]
    cuts = (0, total * 25 // 48 // (16 * packing) * (16 * packing), total)
    table_t = item_table.T
    found = lookup(item_ids, group_counts, table_t, cuts)
    pieces = [
        lax.all_to_all(chunk, "table", split_axis=0, concat_axis=0, tiled=True) for chunk in found
    ]
    history = gather_history(history)
    weights = (w_in, w_out, w_proj, w_back)
    states = []
    for low, chunk in zip(cuts, pieces):
        before = states if low == cuts[-2] else []
        states = states + [
            rank(group_counts, lengths, chunk, before, history, weights, low, capacity)
        ]
    return states[-1]


def solution(mesh):
    placed = (
        P("seq"),
        P("seq", "table"),
        P(),
        P(),
        P("table", None, None, "seq", None),
        P(),
        P(),
        P(),
        P(),
    )
    return jax.shard_map(
        local, mesh=mesh, in_specs=placed, out_specs=P(("table", "seq"), None), check_vma=False
    )
```
